128 devices in a mesh: snp: 16 (over x, y_lo, core), ind: 8 (over y_hi, z).
Axes of the slice: x: 4, y: 4 (y_hi: 2, y_lo: 2; y = y_hi * 2 + y_lo), z: 4, core: 2. Of those that a mesh axis runs over, the one named last changes fastest.
Arguments:
- dosages: bfloat16 [32768, 16384], P('ind', 'snp'), may hold values from -6 to 6
- window_end: int32 [32], P('snp'), may hold values from 0 to 31, as said below
Outputs:
- ld_band: float32 [32, 5, 512, 512], P('snp', None, 'ind')
- ld_mirror: float32 [32, 5, 512, 512], P('snp', None, 'ind')
The draws below stay inside these ranges and needn't reach their ends.
Inputs may be any that keep to these rules, and one draw needn't show every extreme that they name: window_end[i] lies between i and i + 4, and never past 32 - 1; block 0's window reaches exactly 4 blocks ahead.
All inputs are finite; a program needn't handle non-finite values.
Results may differ from the reference program's by a relative error of at most 0.0003.
Values may be sent and summed in bfloat16 or wider, within the bound.
A program may use at most 128 MiB of HBM per device.

```python
import jax
import jax.numpy as jnp
from jax import lax

BLOCK = 512
OFFS = 5
NBLOCKS = 32
NSNP = 16384
IND = 32768


def draw_window_end(key, part):
    key = jax.random.fold_in(key, 7)
    first_key, second_key = jax.random.split(key)
    first_span = jax.random.randint(first_key, (NBLOCKS,), 0, OFFS)
    second_span = jax.random.randint(second_key, (NBLOCKS,), 0, OFFS)
    span = jnp.minimum(first_span, second_span)
    positions = jnp.arange(NBLOCKS, dtype=jnp.int32)
    span = jnp.where(positions == 0, OFFS - 1, span)
    return jnp.minimum(positions + span, NBLOCKS - 1).astype(jnp.int32)


def shard_levels(stream_key, dims, pieces, smallest, top_value):
    def one(dim, parts):
        steps = jax.random.uniform(jax.random.fold_in(jax.random.fold_in(stream_key, 6), dim), (parts,), jnp.float32, smallest / len(pieces), top_value / len(pieces))
        return jnp.repeat(jnp.exp(steps), dims[dim] // parts).reshape((-1,) + (1,) * (len(dims) - dim - 1))

    level = one(*pieces[0])
    for cut in pieces[1:]:
        level = level * one(*cut)
    return level


def bell_draw(key, shape, spread, limit, shards=(), held_as=jnp.bfloat16):
    array = spread * jax.random.normal(key, shape, jnp.float32)
    if shards:
        array = array * shard_levels(key, shape, shards, -0.22, 0.18)
    return jnp.clip(array, -limit, limit).astype(held_as)


def setup_inputs(seed: int = 0) -> dict:
    key_list = jax.random.split(jax.random.key(seed), 3)
    return {
        "dosages": bell_draw(key_list[0], (IND, NSNP), 1.0, 6.0, ((0, 8), (1, 16))),
        "window_end": draw_window_end(jax.random.fold_in(key_list[2], 71), 0),
    }


def reference(dosages, window_end):
    count = dosages.shape[0]

    def one_block(index):
        left_block = lax.dynamic_slice_in_dim(dosages, index * BLOCK, BLOCK, 1).astype(jnp.float32)
        tile_list = []
        for offset in range(OFFS):
            partner = jnp.minimum(index + offset, NBLOCKS - 1).astype(jnp.int32)
            right_block = lax.dynamic_slice_in_dim(dosages, partner * BLOCK, BLOCK, 1).astype(jnp.float32)
            tile_value = jnp.dot(left_block.T, right_block, precision=lax.Precision.HIGHEST, preferred_element_type=jnp.float32) / float(count)
            is_valid = (index + offset) <= window_end[index]
            tile_list.append(jnp.where(is_valid, tile_value, jnp.float32(0.0)))
        return jnp.stack(tile_list)

    ld_band = lax.map(one_block, jnp.arange(NBLOCKS, dtype=jnp.int32))
    mirror_list = []
    for offset in range(OFFS):
        turned = jnp.swapaxes(ld_band[:, offset], 1, 2)
        shifted = jnp.concatenate([jnp.zeros((offset, BLOCK, BLOCK), jnp.float32), turned[:NBLOCKS - offset]], axis=0)
        mirror_list.append(shifted)
    ld_mirror = jnp.stack(mirror_list, axis=1)
    return ld_band, ld_mirror
```

```python
import functools

import jax
import jax.numpy as jnp
from jax import lax
from jax.experimental import pallas as pl
from jax.experimental.pallas import tpu as pltpu
from jax.sharding import PartitionSpec as P

MESH = pl.DeviceIdType.MESH
F32 = jnp.float32
RANKS = 8
DEVS = 16
CHUNK = 512
AHEAD = 4


def both(condition, then, otherwise):
    pl.when(condition)(then)
    pl.when(jnp.logical_not(condition))(otherwise)


def kernel(right_blocks, left_blocks, pick_ref, x_ref, band, mirror, *refs):
    names = list(scratch(right_blocks, left_blocks))
    r = dict(zip(names, refs))
    xb, q, stage = r["xb"], r["q"], r["stage"]
    snp, ind = lax.axis_index("snp"), lax.axis_index("ind")
    odd = lax.rem(snp, 2) == 1
    even = jnp.logical_not(odd)
    parity = lax.rem(snp, 2)
    partner = snp + 1 - 2 * parity
    across = snp - 1 + 2 * parity
    has_q = jnp.logical_and(across >= 0, across < DEVS)
    across = jnp.clip(across, 0, DEVS - 1)
    hi, z = ind // 4, lax.rem(ind, 4)
    chunks = x_ref.shape[0] // CHUNK
    width = x_ref.shape[1] // 2

    loads = []
    for block in range(2):
        load = pltpu.make_async_copy(x_ref.at[:, pl.ds(block * width, width)], xb.at[block], r["load_sem"].at[block])
        load.start()
        loads.append(load)
    band[...] = jnp.zeros_like(band)
    mirror[...] = jnp.zeros_like(mirror)

    barrier = pltpu.get_barrier_semaphore()

    @pl.loop(0, RANKS)
    def _(other):
        pl.semaphore_signal(barrier, inc=1, device_id=(partner, other), device_id_type=MESH)

        @pl.when(other != ind)
        def _():
            pl.semaphore_signal(barrier, inc=1, device_id=(snp, other), device_id_type=MESH)

    @pl.when(has_q)
    def _():
        pl.semaphore_signal(barrier, inc=1, device_id=(across, ind), device_id_type=MESH)

    both(
        has_q,
        lambda: pl.semaphore_wait(barrier, 2 * RANKS),
        lambda: pl.semaphore_wait(barrier, 2 * RANKS - 1),
    )
    for load in loads:
        load.wait()

    pieces = [(n, s) for n in range(max(right_blocks, left_blocks)) for s in range(2)]

    def sends(n):
        return has_q if n < min(right_blocks, left_blocks) else jnp.logical_and(has_q, odd if right_blocks > n else even)

    def receives(n):
        return has_q if n < min(right_blocks, left_blocks) else jnp.logical_and(has_q, even if right_blocks > n else odd)

    def halo(n, s, c):
        rows = pl.ds(pl.multiple_of(c * CHUNK, CHUNK), CHUNK)
        half = jnp.where(odd, s, 1 - s)
        cols = pl.ds(pl.multiple_of(half * (width // 2), width // 2), width // 2)
        if right_blocks == 1:
            src = stage.at[rows, cols]
        else:
            src = xb.at[jnp.where(odd, 1 - n, n), rows, cols]
        at = (n * 2 + s) * chunks + c
        return pltpu.make_async_remote_copy(
            src, q.at[n, s, rows], r["halo_send"].at[at], r["halo_recv"].at[at], device_id=(across, ind), device_id_type=MESH
        )

    def start_halo(number):
        n, s, c = number // (2 * chunks), number // chunks % 2, number % chunks
        pl.when(sends(n))(lambda: halo(n, s, c).start())

    swap = [
        pltpu.make_async_remote_copy(
            xb.at[block], xb.at[2 + block], r["swap_send"].at[block], r["swap_recv"].at[block],
            device_id=(partner, ind), device_id_type=MESH,
        )
        for block in range(2)
    ]

    if right_blocks == 1:
        picked = jnp.where(odd, pick_ref[0], 0)
        for c in range(chunks):
            rows = pl.ds(c * CHUNK, CHUNK)
            stage[rows, :] = xb[picked, rows, :]
    for number in range(AHEAD):
        start_halo(number)
    for copy in swap:
        copy.start()

    def half_of(s):
        return jnp.where(odd, 1 - s, s)

    def tile(acc, s, t, a, b):
        cols = pl.ds(pl.multiple_of(half_of(s) * (width // 2), width // 2), width // 2)
        acc[s, :, t] = jnp.zeros((4, 64, width), F32)

        @pl.loop(0, xb.shape[1] // 1024)
        def _(k):
            rows = pl.ds(pl.multiple_of(k * 1024, 1024), 1024)
            product = lax.dot_general(
                xb[a, rows, cols], xb[b, rows, :], (((0,), (0,)), ((), ())), preferred_element_type=F32
            )
            acc[s, :, t] += product.reshape(4, 64, width)

    class Family:
        def __init__(self, name, number):
            self.number, self.name = number, name
            self.acc, self.zr, self.red, self.yr, self.rt, self.mt = (r[name + k] for k in ("acc", "zr", "red", "yr", "rt", "mt"))

        def z_copy(self, s, k):
            other = lax.rem(z + k, 4)
            at = self.number * 6 + s * 3 + k - 1
            return pltpu.make_async_remote_copy(
                self.acc.at[s, other], self.zr.at[s, 3 - k], r["z_send"].at[at], r["z_recv"].at[at],
                device_id=(snp, hi * 4 + other), device_id_type=MESH,
            )

        def z_start(self, s):
            for k in range(1, 4):
                self.z_copy(s, k).start()

        def y_copy(self, s):
            return pltpu.make_async_remote_copy(
                self.red.at[s], self.yr, r["y_send"].at[self.number], r["y_recv"].at[self.number],
                device_id=(snp, (1 - hi) * 4 + z), device_id_type=MESH,
            )

        def z_finish(self, s):
            for k in range(1, 4):
                self.z_copy(s, k).wait_recv()
            self.red[s] = self.acc[s, z] + self.zr[s, 0] + self.zr[s, 1] + self.zr[s, 2]
            pl.when(hi != half_of(s))(lambda: self.y_copy(s).start())

        def y_finish(self, s, packs, then):
            @pl.when(hi == half_of(s))
            def _():
                self.y_copy(s).wait_recv()
                self.yr[...] = self.yr[...] + self.red[s]
                for p, (t, u) in enumerate(packs):
                    pair = jnp.concatenate([self.yr[t], self.yr[u]], axis=0)
                    self.rt[:, p] = pair.T.reshape(RANKS, 64, 128)
                then()

        def drain(self):
            for s in range(2):
                for k in range(1, 4):
                    self.z_copy(s, k).wait_send()
            for s in range(2):
                pl.when(hi != half_of(s))(lambda: self.y_copy(s).wait_send())

        def pack_copy(self, p, kind, device, other, source):
            return pltpu.make_async_remote_copy(
                self.rt.at[other, p], self.mt.at[kind, source],
                r["pack_send"].at[(self.number * 3 + kind) * RANKS + other],
                r["pack_recv"].at[(self.number * 3 + kind) * RANKS + source],
                device_id=(device, other), device_id_type=MESH,
            )

        def pack_send(self, p, kind, to_self):
            @pl.loop(0, RANKS)
            def _(other):
                if to_self:
                    pl.when(other != ind)(lambda: self.pack_copy(p, kind, snp, other, ind).start())
                else:
                    self.pack_copy(p, kind, partner, other, ind).start()

            if to_self:
                self.mt[kind, ind] = self.rt[ind, p]

        def pack_drain(self, p, kind, to_self):
            @pl.loop(0, RANKS)
            def _(other):
                if to_self:
                    pl.when(other != ind)(lambda: self.pack_copy(p, kind, snp, other, ind).wait_send())
                else:
                    self.pack_copy(p, kind, partner, other, ind).wait_send()

        def pack_wait(self, kind, from_self):
            @pl.loop(0, RANKS)
            def _(source):
                if from_self:
                    pl.when(source != ind)(lambda: self.pack_copy(0, kind, snp, 0, source).wait_recv())
                else:
                    self.pack_copy(0, kind, partner, 0, source).wait_recv()

        def turned(self, kind, side):
            lanes = slice(64 * side, 64 * side + 64)
            return jnp.concatenate([self.mt[kind, source][:, lanes] for source in range(RANKS)], axis=1)

    inner, near = Family("i", 0), Family("a", 1)
    far = Family("b", 2) if max(right_blocks, left_blocks) == 2 else None

    def forward(at, src, dst, device):
        return pltpu.make_async_remote_copy(
            src, dst, r["fwd_send"].at[at], r["fwd_recv"].at[at], device_id=(device, ind), device_id_type=MESH
        )

    fwd_inner = lambda: forward(0, inner.yr.at[pl.ds(3, 2)], band.at[1, pl.ds(1, 2)], partner)
    fwd_even_one = lambda: forward(1, near.yr.at[0], band.at[1, 2], across)
    fwd_even_two = lambda: forward(2, near.yr.at[pl.ds(2, 2)], band.at[1, pl.ds(3, 2)], across)
    fwd_odd = lambda: forward(3, near.yr, mirror.at[0, pl.ds(1, 4)], across)
    fwd_even_far = lambda: forward(4, far.yr, band.at[0, pl.ds(3, 2)], across)
    fwd_odd_far = lambda: forward(5, far.yr.at[1], mirror.at[1, 4], across)

    def inner_places():
        band[0, 0] = inner.yr[0]
        mirror[0, 0] = inner.yr[0]
        band[1, 0] = inner.yr[1]
        mirror[1, 0] = inner.yr[1]
        band[0, 1] = inner.yr[2]
        inner.pack_send(0, 0, True)

        @pl.when(odd)
        def _():
            fwd_inner().start()
            inner.pack_send(1, 1, True)

        @pl.when(even)
        def _():
            band[0, 2] = inner.yr[3]
            band[0, 3] = inner.yr[4]
            inner.pack_send(1, 2, False)

    def near_places():
        @pl.when(odd)
        def _():
            fwd_odd().start()

        @pl.when(even)
        def _():
            fwd_even_one().start()
            fwd_even_two().start()

        near.pack_send(0, 0, True)
        near.pack_send(1, 1, False)

    def far_places():
        @pl.when(even)
        def _():
            fwd_even_far().start()
            far.pack_send(0, 0, True)

        @pl.when(odd)
        def _():
            fwd_odd_far().start()

        far.pack_send(1, 1, False)

    def inner_tiles(s, waits):
        tile(inner.acc, s, 0, 0, 0)
        tile(inner.acc, s, 1, 1, 1)
        tile(inner.acc, s, 2, 0, 1)
        for copy in waits:
            copy.wait_recv()
        tile(inner.acc, s, 3, jnp.where(odd, 3, 0), jnp.where(odd, 0, 2))
        tile(inner.acc, s, 4, jnp.where(odd, 3, 0), jnp.where(odd, 1, 3))
        inner.z_start(s)

    inner_tiles(0, swap)
    inner_tiles(1, ())

    def cross(n, s, family, slots, first, last):
        acc = family.acc
        if first == 0:
            acc[s] = jnp.zeros(acc.shape[1:], F32)

        @pl.when(receives(n))
        def _():
            @pl.loop(first, last)
            def _(c):
                halo(n, s, c).wait_recv()
                rows = pl.ds(pl.multiple_of(c * CHUNK, CHUNK), CHUNK)
                left = q[n, s, rows, :]
                for t, b in enumerate(slots):
                    product = lax.dot_general(
                        left, xb[b, rows, :], (((0,), (0,)), ((), ())), preferred_element_type=F32
                    )
                    acc[s, :, t] += product.reshape(4, 64, width)

    total = len(pieces) * chunks

    def cross_step(index, first, last):
        n, s = pieces[index]
        family = near if n == 0 else far
        slots = near_slots if n == 0 else far_slots
        for c in range(first, last):
            cross(n, s, family, slots, c, c + 1)
            number = index * chunks + c
            pl.when(sends(n))(lambda: halo(n, s, c).wait_send())
            if number + AHEAD < total:
                start_halo(number + AHEAD)
        if last == chunks:
            pl.when(receives(n))(lambda: family.z_start(s))

    near_slots = [1, 0, jnp.where(odd, 3, 2), jnp.where(odd, 2, 3)]
    far_slots = [1, jnp.where(odd, 3, 2)]
    steps = [(index, first, first + chunks // 2) for index in range(len(pieces)) for first in (0, chunks // 2)]
    for number, step in enumerate(steps):
        cross_step(*step)
        if number == 1:
            inner.z_finish(0)
        if number == 2:
            inner.y_finish(0, [(2, 2), (3, 4)], inner_places)
            inner.z_finish(1)
        if number == 3:
            inner.y_finish(1, [(2, 2), (3, 4)], inner_places)
            pl.when(has_q)(lambda: near.z_finish(0))
        if number == 4:
            pl.when(has_q)(lambda: near.y_finish(0, [(0, 1), (2, 3)], near_places))
        if number == 5:
            pl.when(has_q)(lambda: near.z_finish(1))
        if number == 6:
            pl.when(has_q)(lambda: near.y_finish(1, [(0, 1), (2, 3)], near_places))
        if number == 7:
            pl.when(receives(1))(lambda: far.z_finish(0))
    if far is None:
        @pl.when(has_q)
        def _():
            near.y_finish(0, [(0, 1), (2, 3)], near_places)
            near.z_finish(1)
            near.y_finish(1, [(0, 1), (2, 3)], near_places)
    else:
        @pl.when(receives(1))
        def _():
            far.y_finish(0, [(0, 0), (1, 1)], far_places)
            far.z_finish(1)
            far.y_finish(1, [(0, 0), (1, 1)], far_places)

    inner.pack_wait(0, True)
    mirror[1, 1] = inner.turned(0, 0)

    @pl.when(odd)
    def _():
        inner.pack_wait(1, True)
        mirror[0, 1] = inner.turned(1, 0)
        mirror[1, 2] = inner.turned(1, 1)
        inner.pack_wait(2, False)
        mirror[0, 2] = inner.turned(2, 0)
        mirror[1, 3] = inner.turned(2, 1)

    pl.when(even)(lambda: fwd_inner().wait_recv())

    @pl.when(has_q)
    def _():
        near.pack_wait(0, True)

        @pl.when(odd)
        def _():
            fwd_even_one().wait_recv()
            fwd_even_two().wait_recv()
            band[1, 1] = near.turned(0, 0)
            band[0, 2] = near.turned(0, 1)
            if right_blocks == 1:
                band[0, 3] = band[1, 2]
                band[0, 4] = band[1, 3]

        @pl.when(even)
        def _():
            fwd_odd().wait_recv()
            mirror[1, 2] = near.turned(0, 0)
            if right_blocks == 1:
                mirror[1, 3] = near.turned(0, 0)

    partner_q = jnp.where(odd, snp > 1, snp < DEVS - 2)

    @pl.when(partner_q)
    def _():
        near.pack_wait(1, False)

        @pl.when(even)
        def _():
            band[1, 3] = near.turned(1, 0)
            band[0, 4] = near.turned(1, 1)

        @pl.when(odd)
        def _():
            mirror[0, 3] = near.turned(1, 0)
            mirror[1, 4] = near.turned(1, 1)
            if right_blocks == 1:
                mirror[0, 4] = near.turned(1, 0)

    if far is not None:
        @pl.when(jnp.logical_and(has_q, odd))
        def _():
            fwd_even_far().wait_recv()

        if left_blocks == 2:
            @pl.when(jnp.logical_and(has_q, even))
            def _():
                fwd_odd_far().wait_recv()

            @pl.when(jnp.logical_and(partner_q, even))
            def _():
                far.pack_wait(1, False)
                band[1, 4] = far.turned(1, 0)

        @pl.when(jnp.logical_and(has_q, even))
        def _():
            far.pack_wait(0, True)
            mirror[1, 3] = far.turned(0, 0)

        @pl.when(jnp.logical_and(partner_q, odd))
        def _():
            far.pack_wait(1, False)
            mirror[0, 4] = far.turned(1, 0)

    for copy in swap:
        copy.wait_send()
    inner.drain()
    inner.pack_drain(0, 0, True)

    @pl.when(odd)
    def _():
        fwd_inner().wait_send()
        inner.pack_drain(1, 1, True)

    pl.when(even)(lambda: inner.pack_drain(1, 2, False))

    @pl.when(has_q)
    def _():
        near.drain()
        near.pack_drain(0, 0, True)
        near.pack_drain(1, 1, False)

        @pl.when(odd)
        def _():
            fwd_odd().wait_send()

        @pl.when(even)
        def _():
            fwd_even_one().wait_send()
            fwd_even_two().wait_send()

    if far is not None:
        @pl.when(receives(1))
        def _():
            far.drain()
            far.pack_drain(1, 1, False)

            @pl.when(even)
            def _():
                fwd_even_far().wait_send()
                far.pack_drain(0, 0, True)

            @pl.when(odd)
            def _():
                fwd_odd_far().wait_send()


def scratch(right_blocks, left_blocks):
    blocks = max(right_blocks, left_blocks)
    dma = lambda count: pltpu.SemaphoreType.DMA((count,))
    shapes = {
        "xb": pltpu.VMEM((4, 4096, 512), jnp.bfloat16),
        "q": pltpu.VMEM((blocks, 2, 4096, 256), jnp.bfloat16),
        "stage": pltpu.VMEM((4096 if right_blocks == 1 else 16, 512), jnp.bfloat16),
        "load_sem": dma(2),
        "swap_send": dma(2),
        "swap_recv": dma(2),
        "halo_send": dma(blocks * 16),
        "halo_recv": dma(blocks * 16),
        "z_send": dma(18),
        "z_recv": dma(18),
        "y_send": dma(3),
        "y_recv": dma(3),
        "pack_send": dma(72),
        "pack_recv": dma(72),
        "fwd_send": dma(6),
        "fwd_recv": dma(6),
    }
    families = [("i", 5, 3), ("a", 4, 2)] + ([("b", 2, 2)] if blocks == 2 else [])
    for name, count, kinds in families:
        shapes[name + "acc"] = pltpu.VMEM((2, 4, count, 64, 512), F32)
        shapes[name + "zr"] = pltpu.VMEM((2, 3, count, 64, 512), F32)
        shapes[name + "red"] = pltpu.VMEM((2, count, 64, 512), F32)
        shapes[name + "yr"] = pltpu.VMEM((count, 64, 512), F32)
        shapes[name + "rt"] = pltpu.VMEM((RANKS, 2, 64, 128), F32)
        shapes[name + "mt"] = pltpu.VMEM((kinds, RANKS, 64, 128), F32)
    return shapes


def tiles(right_blocks, left_blocks, pick, dosages):
    out = jax.ShapeDtypeStruct((2, 5, 64, 512), F32)
    return pl.pallas_call(
        functools.partial(kernel, right_blocks, left_blocks),
        out_shape=(out, out),
        in_specs=[pl.BlockSpec(memory_space=pltpu.SMEM), pl.BlockSpec(memory_space=pl.ANY)],
        out_specs=(pl.BlockSpec(memory_space=pltpu.VMEM),) * 2,
        scratch_shapes=list(scratch(right_blocks, left_blocks).values()),
        compiler_params=pltpu.CompilerParams(
            collective_id=right_blocks * 2 + left_blocks, has_side_effects=True, vmem_limit_bytes=62 << 20
        ),
        cost_estimate=pl.CostEstimate(flops=21_474_836_480, bytes_accessed=11_000_000, transcendentals=0),
        name=f"tiles_{right_blocks}_{left_blocks}",
    )(pick, dosages)


def local(dosages, window_end):
    windows = lax.all_gather(window_end, "snp", tiled=True)
    first = lax.axis_index("snp") * 2
    block = first + jnp.arange(2, dtype=jnp.int32)[:, None]
    offset = jnp.arange(5, dtype=jnp.int32)[None, :]
    band_valid = block + offset <= window_end[:, None]
    earlier = block - offset
    reach = jnp.sum(
        jnp.where(jnp.arange(32, dtype=jnp.int32) == earlier[..., None], windows, jnp.int32(0)), axis=-1, dtype=jnp.int32
    )
    mirror_valid = jnp.logical_and(earlier >= 0, block <= reach)
    band, mirror = tiles(2, 2, jnp.zeros((1,), jnp.int32), dosages)
    scale = jnp.float32(1.0 / 32768.0)
    band = jnp.where(band_valid[..., None, None], band * scale, jnp.float32(0.0))
    mirror = jnp.where(mirror_valid[..., None, None], mirror * scale, jnp.float32(0.0))
    return band, mirror


def solution(mesh):
    in_specs = (P("ind", "snp"), P("snp"))
    out_specs = (P("snp", None, "ind", None), P("snp", None, "ind", None))
    return jax.shard_map(local, mesh=mesh, in_specs=in_specs, out_specs=out_specs, check_vma=False)
```

```python
import functools

import jax
import jax.numpy as jnp
from jax import lax
from jax.experimental import pallas as pl
from jax.experimental.pallas import tpu as pltpu
from jax.sharding import PartitionSpec as P

MESH = pl.DeviceIdType.MESH
F32 = jnp.float32
RANKS = 8
DEVS = 16
CHUNK = 512
AHEAD = 6


def both(condition, then, otherwise):
    pl.when(condition)(then)
    pl.when(jnp.logical_not(condition))(otherwise)


def kernel(right_blocks, left_blocks, pick_ref, x_ref, band, mirror, *refs):
    names = list(scratch(right_blocks, left_blocks))
    r = dict(zip(names, refs))
    xb, q, stage = r["xb"], r["q"], r["stage"]
    snp, ind = lax.axis_index("snp"), lax.axis_index("ind")
    odd = lax.rem(snp, 2) == 1
    even = jnp.logical_not(odd)
    parity = lax.rem(snp, 2)
    partner = snp + 1 - 2 * parity
    across = snp - 1 + 2 * parity
    has_q = jnp.logical_and(across >= 0, across < DEVS)
    across = jnp.clip(across, 0, DEVS - 1)
    hi, z = ind // 4, lax.rem(ind, 4)
    chunks = x_ref.shape[0] // CHUNK
    width = x_ref.shape[1] // 2

    loads = []
    for block in range(2):
        load = pltpu.make_async_copy(x_ref.at[:, pl.ds(block * width, width)], xb.at[block], r["load_sem"].at[block])
        load.start()
        loads.append(load)
    band[...] = jnp.zeros_like(band)
    mirror[...] = jnp.zeros_like(mirror)

    barrier = pltpu.get_barrier_semaphore()

    @pl.loop(0, RANKS)
    def _(other):
        pl.semaphore_signal(barrier, inc=1, device_id=(partner, other), device_id_type=MESH)

        @pl.when(other != ind)
        def _():
            pl.semaphore_signal(barrier, inc=1, device_id=(snp, other), device_id_type=MESH)

    @pl.when(has_q)
    def _():
        pl.semaphore_signal(barrier, inc=1, device_id=(across, ind), device_id_type=MESH)

    both(
        has_q,
        lambda: pl.semaphore_wait(barrier, 2 * RANKS),
        lambda: pl.semaphore_wait(barrier, 2 * RANKS - 1),
    )
    for load in loads:
        load.wait()

    pieces = [(n, s) for n in range(max(right_blocks, left_blocks)) for s in range(2)]

    def sends(n):
        return has_q if n < min(right_blocks, left_blocks) else jnp.logical_and(has_q, odd if right_blocks > n else even)

    def receives(n):
        return has_q if n < min(right_blocks, left_blocks) else jnp.logical_and(has_q, even if right_blocks > n else odd)

    def halo(n, s, c):
        rows = pl.ds(pl.multiple_of(c * CHUNK, CHUNK), CHUNK)
        half = jnp.where(odd, s, 1 - s)
        cols = pl.ds(pl.multiple_of(half * (width // 2), width // 2), width // 2)
        if right_blocks == 1:
            src = stage.at[rows, cols]
        else:
            src = xb.at[jnp.where(odd, 1 - n, n), rows, cols]
        at = (n * 2 + s) * chunks + c
        return pltpu.make_async_remote_copy(
            src, q.at[n, s, rows], r["halo_send"].at[at], r["halo_recv"].at[at], device_id=(across, ind), device_id_type=MESH
        )

    def start_halo(number):
        n, s, c = number // (2 * chunks), number // chunks % 2, number % chunks
        pl.when(sends(n))(lambda: halo(n, s, c).start())

    swap = [
        pltpu.make_async_remote_copy(
            xb.at[block], xb.at[2 + block], r["swap_send"].at[block], r["swap_recv"].at[block],
            device_id=(partner, ind), device_id_type=MESH,
        )
        for block in range(2)
    ]

    if right_blocks == 1:
        picked = jnp.where(odd, pick_ref[0], 0)
        for c in range(chunks):
            rows = pl.ds(c * CHUNK, CHUNK)
            stage[rows, :] = jnp.where(picked == 1, xb[1, rows, :], xb[0, rows, :])
    for number in range(AHEAD):
        start_halo(number)
    for copy in swap:
        copy.start()

    def half_of(s):
        return jnp.where(odd, 1 - s, s)

    def tile(acc, s, t, a, b):
        cols = pl.ds(pl.multiple_of(half_of(s) * (width // 2), width // 2), width // 2)
        acc[s, :, t] = jnp.zeros((4, 64, width), F32)

        @pl.loop(0, xb.shape[1] // 1024)
        def _(k):
            rows = pl.ds(pl.multiple_of(k * 1024, 1024), 1024)
            product = lax.dot_general(
                xb[a, rows, cols], xb[b, rows, :], (((0,), (0,)), ((), ())), preferred_element_type=F32
            )
            acc[s, :, t] += product.reshape(4, 64, width)

    class Family:
        def __init__(self, name, number, even_count, odd_count):
            self.number, self.name = number, name
            self.even_count, self.odd_count = even_count, odd_count
            self.acc, self.zr, self.red, self.yr, self.rt, self.mt = (r[name + k] for k in ("acc", "zr", "red", "yr", "rt", "mt"))

        def z_copy(self, s, k, count):
            other = lax.rem(z + k, 4)
            at = self.number * 6 + s * 3 + k - 1
            some = pl.ds(0, count)
            return pltpu.make_async_remote_copy(
                self.acc.at[s, other, some], self.zr.at[s, 3 - k, some], r["z_send"].at[at], r["z_recv"].at[at],
                device_id=(snp, hi * 4 + other), device_id_type=MESH,
            )

        def y_copy(self, s, count):
            some = pl.ds(0, count)
            return pltpu.make_async_remote_copy(
                self.red.at[s, some], self.yr.at[some], r["y_send"].at[self.number], r["y_recv"].at[self.number],
                device_id=(snp, (1 - hi) * 4 + z), device_id_type=MESH,
            )

        def by_parity(self, action):
            if self.even_count == self.odd_count:
                action(self.even_count)
            else:
                both(even, lambda: action(self.even_count), lambda: action(self.odd_count))

        def z_start(self, s):
            def action(count):
                for k in range(1, 4):
                    self.z_copy(s, k, count).start()

            self.by_parity(action)

        def z_finish(self, s):
            def action(count):
                for k in range(1, 4):
                    self.z_copy(s, k, count).wait_recv()
                self.red[s, :count] = self.acc[s, z, :count] + self.zr[s, 0, :count] + self.zr[s, 1, :count] + self.zr[s, 2, :count]
                pl.when(hi != half_of(s))(lambda: self.y_copy(s, count).start())

            self.by_parity(action)

        def y_finish(self, s, packs, then):
            @pl.when(hi == half_of(s))
            def _():
                def action(count):
                    self.y_copy(s, count).wait_recv()
                    self.yr[:count] = self.yr[:count] + self.red[s, :count]

                self.by_parity(action)
                for p, (t, u) in enumerate(packs):
                    pair = jnp.concatenate([self.yr[t], self.yr[u]], axis=0)
                    self.rt[:, p] = pair.T.reshape(RANKS, 64, 128)
                then()

        def drain(self):
            def action(count):
                for s in range(2):
                    for k in range(1, 4):
                        self.z_copy(s, k, count).wait_send()
                for s in range(2):
                    pl.when(hi != half_of(s))(lambda: self.y_copy(s, count).wait_send())

            self.by_parity(action)

        def pack_copy(self, p, kind, device, other, source):
            return pltpu.make_async_remote_copy(
                self.rt.at[other, p], self.mt.at[kind, source],
                r["pack_send"].at[(self.number * 3 + kind) * RANKS + other],
                r["pack_recv"].at[(self.number * 3 + kind) * RANKS + source],
                device_id=(device, other), device_id_type=MESH,
            )

        def pack_send(self, p, kind, to_self):
            @pl.loop(0, RANKS)
            def _(other):
                if to_self:
                    pl.when(other != ind)(lambda: self.pack_copy(p, kind, snp, other, ind).start())
                else:
                    self.pack_copy(p, kind, partner, other, ind).start()

            if to_self:
                self.mt[kind, ind] = self.rt[ind, p]

        def pack_drain(self, p, kind, to_self):
            @pl.loop(0, RANKS)
            def _(other):
                if to_self:
                    pl.when(other != ind)(lambda: self.pack_copy(p, kind, snp, other, ind).wait_send())
                else:
                    self.pack_copy(p, kind, partner, other, ind).wait_send()

        def pack_wait(self, kind, from_self):
            @pl.loop(0, RANKS)
            def _(source):
                if from_self:
                    pl.when(source != ind)(lambda: self.pack_copy(0, kind, snp, 0, source).wait_recv())
                else:
                    self.pack_copy(0, kind, partner, 0, source).wait_recv()

        def turned(self, kind, side):
            lanes = slice(64 * side, 64 * side + 64)
            return jnp.concatenate([self.mt[kind, source][:, lanes] for source in range(RANKS)], axis=1)

    inner, near = Family("i", 0, 5, 5), Family("a", 1, 3, 4)
    far = Family("b", 2, 2, 2) if max(right_blocks, left_blocks) == 2 else None

    def forward(at, src, dst, device):
        return pltpu.make_async_remote_copy(
            src, dst, r["fwd_send"].at[at], r["fwd_recv"].at[at], device_id=(device, ind), device_id_type=MESH
        )

    fwd_inner = lambda: forward(0, inner.yr.at[pl.ds(3, 2)], band.at[1, pl.ds(1, 2)], partner)
    fwd_even = lambda: forward(1, near.yr.at[pl.ds(0, 3)], band.at[1, pl.ds(2, 3)], across)
    fwd_odd = lambda: forward(3, near.yr, mirror.at[0, pl.ds(1, 4)], across)
    fwd_even_far = lambda: forward(4, far.yr, band.at[0, pl.ds(3, 2)], across)
    fwd_odd_far = lambda: forward(5, far.yr.at[1], mirror.at[1, 4], across)

    def inner_places():
        band[0, 0] = inner.yr[0]
        mirror[0, 0] = inner.yr[0]
        band[1, 0] = inner.yr[1]
        mirror[1, 0] = inner.yr[1]
        band[0, 1] = inner.yr[2]
        inner.pack_send(0, 0, True)

        @pl.when(odd)
        def _():
            fwd_inner().start()
            inner.pack_send(1, 1, True)

        @pl.when(even)
        def _():
            band[0, 2] = inner.yr[3]
            band[0, 3] = inner.yr[4]
            inner.pack_send(1, 2, False)

    def near_places():
        @pl.when(odd)
        def _():
            fwd_odd().start()

        @pl.when(even)
        def _():
            fwd_even().start()

        near.pack_send(0, 0, True)
        near.pack_send(1, 1, False)

    def far_places():
        @pl.when(even)
        def _():
            fwd_even_far().start()
            far.pack_send(0, 0, True)

        @pl.when(odd)
        def _():
            fwd_odd_far().start()

        far.pack_send(1, 1, False)

    def inner_tiles(s, waits):
        tile(inner.acc, s, 0, 0, 0)
        tile(inner.acc, s, 1, 1, 1)
        tile(inner.acc, s, 2, 0, 1)
        for copy in waits:
            copy.wait_recv()
        tile(inner.acc, s, 3, jnp.where(odd, 3, 0), jnp.where(odd, 0, 2))
        tile(inner.acc, s, 4, jnp.where(odd, 3, 0), jnp.where(odd, 1, 3))
        inner.z_start(s)

    inner_tiles(0, swap)
    inner_tiles(1, ())

    def cross(n, s, family, slots, first, last):
        acc = family.acc
        if first == 0:
            acc[s] = jnp.zeros(acc.shape[1:], F32)

        @pl.when(receives(n))
        def _():
            @pl.loop(first, last)
            def _(c):
                halo(n, s, c).wait_recv()
                rows = pl.ds(pl.multiple_of(c * CHUNK, CHUNK), CHUNK)
                left = q[n, s, rows, :]

                def add(t, b):
                    product = lax.dot_general(
                        left, xb[b, rows, :], (((0,), (0,)), ((), ())), preferred_element_type=F32
                    )
                    acc[s, :, t] += product.reshape(4, 64, width)

                for t, b in enumerate(slots):
                    if t < family.even_count:
                        add(t, b)
                    else:
                        pl.when(odd)(lambda: add(t, b))

    total = len(pieces) * chunks

    def cross_step(index, first, last):
        n, s = pieces[index]
        family = near if n == 0 else far
        slots = near_slots if n == 0 else far_slots
        for c in range(first, last):
            cross(n, s, family, slots, c, c + 1)
            number = index * chunks + c
            pl.when(sends(n))(lambda: halo(n, s, c).wait_send())
            if number + AHEAD < total:
                start_halo(number + AHEAD)
        if last == chunks:
            pl.when(receives(n))(lambda: family.z_start(s))

    near_packs = [(0, jnp.where(odd, 1, 0)), (jnp.where(odd, 2, 1), jnp.where(odd, 3, 2))]
    near_slots = [1, jnp.where(odd, 0, 2), 3, 2]
    far_slots = [1, jnp.where(odd, 3, 2)]
    steps = [(index, first, first + chunks // 2) for index in range(len(pieces)) for first in (0, chunks // 2)]
    for number, step in enumerate(steps):
        cross_step(*step)
        if number == 1:
            inner.z_finish(0)
        if number == 2:
            inner.y_finish(0, [(2, 2), (3, 4)], inner_places)
            inner.z_finish(1)
        if number == 3:
            inner.y_finish(1, [(2, 2), (3, 4)], inner_places)
            pl.when(has_q)(lambda: near.z_finish(0))
        if number == 4:
            pl.when(has_q)(lambda: near.y_finish(0, near_packs, near_places))
        if number == 5:
            pl.when(has_q)(lambda: near.z_finish(1))
        if number == 6:
            pl.when(has_q)(lambda: near.y_finish(1, near_packs, near_places))
        if number == 7:
            pl.when(receives(1))(lambda: far.z_finish(0))
    if far is None:
        @pl.when(has_q)
        def _():
            near.y_finish(0, near_packs, near_places)
            near.z_finish(1)
            near.y_finish(1, near_packs, near_places)
    else:
        @pl.when(receives(1))
        def _():
            far.y_finish(0, [(0, 0), (1, 1)], far_places)
            far.z_finish(1)
            far.y_finish(1, [(0, 0), (1, 1)], far_places)

    inner.pack_wait(0, True)
    mirror[1, 1] = inner.turned(0, 0)

    @pl.when(odd)
    def _():
        inner.pack_wait(1, True)
        mirror[0, 1] = inner.turned(1, 0)
        mirror[1, 2] = inner.turned(1, 1)
        inner.pack_wait(2, False)
        mirror[0, 2] = inner.turned(2, 0)
        mirror[1, 3] = inner.turned(2, 1)

    pl.when(even)(lambda: fwd_inner().wait_recv())

    @pl.when(has_q)
    def _():
        near.pack_wait(0, True)

        @pl.when(odd)
        def _():
            fwd_even().wait_recv()
            band[1, 1] = near.turned(0, 0)
            band[0, 2] = near.turned(0, 1)
            if right_blocks == 1:
                band[0, 3] = band[1, 2]
                band[0, 4] = band[1, 3]

        @pl.when(even)
        def _():
            fwd_odd().wait_recv()
            mirror[1, 2] = near.turned(0, 0)
            if right_blocks == 1:
                mirror[1, 3] = near.turned(0, 0)

    partner_q = jnp.where(odd, snp > 1, snp < DEVS - 2)

    @pl.when(partner_q)
    def _():
        near.pack_wait(1, False)

        @pl.when(even)
        def _():
            band[1, 3] = near.turned(1, 0)
            band[0, 4] = near.turned(1, 1)

        @pl.when(odd)
        def _():
            mirror[0, 3] = near.turned(1, 0)
            mirror[1, 4] = near.turned(1, 1)
            if right_blocks == 1:
                mirror[0, 4] = near.turned(1, 0)

    if far is not None:
        @pl.when(jnp.logical_and(has_q, odd))
        def _():
            fwd_even_far().wait_recv()

        if left_blocks == 2:
            @pl.when(jnp.logical_and(has_q, even))
            def _():
                fwd_odd_far().wait_recv()

            @pl.when(jnp.logical_and(partner_q, even))
            def _():
                far.pack_wait(1, False)
                band[1, 4] = far.turned(1, 0)

        @pl.when(jnp.logical_and(has_q, even))
        def _():
            far.pack_wait(0, True)
            mirror[1, 3] = far.turned(0, 0)

        @pl.when(jnp.logical_and(partner_q, odd))
        def _():
            far.pack_wait(1, False)
            mirror[0, 4] = far.turned(1, 0)

    for copy in swap:
        copy.wait_send()
    inner.drain()
    inner.pack_drain(0, 0, True)

    @pl.when(odd)
    def _():
        fwd_inner().wait_send()
        inner.pack_drain(1, 1, True)

    pl.when(even)(lambda: inner.pack_drain(1, 2, False))

    @pl.when(has_q)
    def _():
        near.drain()
        near.pack_drain(0, 0, True)
        near.pack_drain(1, 1, False)

        @pl.when(odd)
        def _():
            fwd_odd().wait_send()

        @pl.when(even)
        def _():
            fwd_even().wait_send()

    if far is not None:
        @pl.when(receives(1))
        def _():
            far.drain()
            far.pack_drain(1, 1, False)

            @pl.when(even)
            def _():
                fwd_even_far().wait_send()
                far.pack_drain(0, 0, True)

            @pl.when(odd)
            def _():
                fwd_odd_far().wait_send()


def scratch(right_blocks, left_blocks):
    blocks = max(right_blocks, left_blocks)
    dma = lambda count: pltpu.SemaphoreType.DMA((count,))
    shapes = {
        "xb": pltpu.VMEM((4, 4096, 512), jnp.bfloat16),
        "q": pltpu.VMEM((blocks, 2, 4096, 256), jnp.bfloat16),
        "stage": pltpu.VMEM((4096 if right_blocks == 1 else 16, 512), jnp.bfloat16),
        "load_sem": dma(2),
        "swap_send": dma(2),
        "swap_recv": dma(2),
        "halo_send": dma(blocks * 16),
        "halo_recv": dma(blocks * 16),
        "z_send": dma(18),
        "z_recv": dma(18),
        "y_send": dma(3),
        "y_recv": dma(3),
        "pack_send": dma(72),
        "pack_recv": dma(72),
        "fwd_send": dma(6),
        "fwd_recv": dma(6),
    }
    families = [("i", 5, 3), ("a", 4, 2)] + ([("b", 2, 2)] if blocks == 2 else [])
    for name, count, kinds in families:
        shapes[name + "acc"] = pltpu.VMEM((2, 4, count, 64, 512), F32)
        shapes[name + "zr"] = pltpu.VMEM((2, 3, count, 64, 512), F32)
        shapes[name + "red"] = pltpu.VMEM((2, count, 64, 512), F32)
        shapes[name + "yr"] = pltpu.VMEM((count, 64, 512), F32)
        shapes[name + "rt"] = pltpu.VMEM((RANKS, 2, 64, 128), F32)
        shapes[name + "mt"] = pltpu.VMEM((kinds, RANKS, 64, 128), F32)
    return shapes


def tiles(right_blocks, left_blocks, pick, dosages):
    out = jax.ShapeDtypeStruct((2, 5, 64, 512), F32)
    return pl.pallas_call(
        functools.partial(kernel, right_blocks, left_blocks),
        out_shape=(out, out),
        in_specs=[pl.BlockSpec(memory_space=pltpu.SMEM), pl.BlockSpec(memory_space=pl.ANY)],
        out_specs=(pl.BlockSpec(memory_space=pltpu.VMEM),) * 2,
        scratch_shapes=list(scratch(right_blocks, left_blocks).values()),
        compiler_params=pltpu.CompilerParams(
            collective_id=right_blocks * 2 + left_blocks, has_side_effects=True, vmem_limit_bytes=62 << 20
        ),
        cost_estimate=pl.CostEstimate(flops=21_474_836_480, bytes_accessed=11_000_000, transcendentals=0),
        name=f"tiles_{right_blocks}_{left_blocks}",
    )(pick, dosages)


def gather_kernel(ends_ref, all_ref, mine, send_sem, recv_sem):
    snp, ind = lax.axis_index("snp"), lax.axis_index("ind")
    barrier = pltpu.get_barrier_semaphore()

    def copy(k):
        other = lax.rem(snp + k, DEVS)
        return pltpu.make_async_remote_copy(
            mine, all_ref.at[snp], send_sem.at[k], recv_sem.at[k], device_id=(other, ind), device_id_type=MESH
        )

    @pl.loop(1, DEVS)
    def _(k):
        pl.semaphore_signal(barrier, inc=1, device_id=(lax.rem(snp + k, DEVS), ind), device_id_type=MESH)

    lane = lax.broadcasted_iota(jnp.int32, (8, 128), 1)
    mine[...] = jnp.where(lane == 0, ends_ref[0], ends_ref[1])
    all_ref[snp] = mine[...]
    pl.semaphore_wait(barrier, DEVS - 1)

    @pl.loop(1, DEVS)
    def _(k):
        copy(k).start()

    @pl.loop(1, DEVS)
    def _(k):
        copy(k).wait()


def gather(window_end):
    everything = pl.pallas_call(
        gather_kernel,
        out_shape=jax.ShapeDtypeStruct((DEVS, 8, 128), jnp.int32),
        in_specs=[pl.BlockSpec(memory_space=pltpu.SMEM)],
        out_specs=pl.BlockSpec(memory_space=pltpu.VMEM),
        scratch_shapes=[
            pltpu.VMEM((8, 128), jnp.int32),
            pltpu.SemaphoreType.DMA((DEVS,)),
            pltpu.SemaphoreType.DMA((DEVS,)),
        ],
        compiler_params=pltpu.CompilerParams(collective_id=1, has_side_effects=True),
        name="gather_ends",
    )(window_end)
    return everything[:, 0, :2].reshape(-1)


def local(dosages, window_end):
    windows = gather(window_end)
    first = lax.axis_index("snp") * 2
    block = first + jnp.arange(2, dtype=jnp.int32)[:, None]
    offset = jnp.arange(5, dtype=jnp.int32)[None, :]
    band_valid = block + offset <= window_end[:, None]
    earlier = block - offset
    reach = jnp.sum(
        jnp.where(jnp.arange(32, dtype=jnp.int32) == earlier[..., None], windows, jnp.int32(0)), axis=-1, dtype=jnp.int32
    )
    mirror_valid = jnp.logical_and(earlier >= 0, block <= reach)

    reaches = (windows.reshape(8, 4) - (4 * jnp.arange(8, dtype=jnp.int32)[:, None] + 3))[:7]
    second_ok = jnp.all(reaches[:, 1] <= 1)
    one_row_ok = jnp.logical_and(second_ok, jnp.all(jnp.minimum(reaches[:, 2], reaches[:, 3]) <= 1))
    choice = jnp.where(one_row_ok, 0, jnp.where(second_ok, 1, 2)).astype(jnp.int32)
    pick = (window_end[1] >= window_end[0]).astype(jnp.int32).reshape(1)
    scale = jnp.float32(1.0 / 32768.0)

    def plan(right_blocks, left_blocks):
        def run(pick, dosages, band_valid, mirror_valid):
            band, mirror = tiles(right_blocks, left_blocks, pick, dosages)
            band = jnp.where(band_valid[..., None, None], band * scale, jnp.float32(0.0))
            mirror = jnp.where(mirror_valid[..., None, None], mirror * scale, jnp.float32(0.0))
            return lax.optimization_barrier((band, mirror))

        return run

    plans = [plan(1, 1), plan(2, 1), plan(2, 2)]
    band, mirror = lax.switch(choice, plans, pick, dosages, band_valid, mirror_valid)
    return band, mirror


def solution(mesh):
    in_specs = (P("ind", "snp"), P("snp"))
    out_specs = (P("snp", None, "ind", None), P("snp", None, "ind", None))
    return jax.shard_map(local, mesh=mesh, in_specs=in_specs, out_specs=out_specs, check_vma=False)
```

```python
import functools

import jax
import jax.numpy as jnp
from jax import lax
from jax.experimental import pallas as pl
from jax.experimental.pallas import tpu as pltpu
from jax.sharding import PartitionSpec as P

MESH = pl.DeviceIdType.MESH
F32 = jnp.float32
RANKS = 8
DEVS = 16
CHUNK = 512


def both(condition, then, otherwise):
    pl.when(condition)(then)
    pl.when(jnp.logical_not(condition))(otherwise)


def kernel(right_blocks, left_blocks, pick_ref, x_ref, band, mirror, *refs):
    names = list(scratch(right_blocks, left_blocks))
    r = dict(zip(names, refs))
    xb, q, stage = r["xb"], r["q"], r["stage"]
    snp, ind = lax.axis_index("snp"), lax.axis_index("ind")
    odd = lax.rem(snp, 2) == 1
    even = jnp.logical_not(odd)
    parity = lax.rem(snp, 2)
    partner = snp + 1 - 2 * parity
    across = snp - 1 + 2 * parity
    has_q = jnp.logical_and(across >= 0, across < DEVS)
    across = jnp.clip(across, 0, DEVS - 1)
    beyond = snp + 2 - 4 * parity
    has_beyond = jnp.logical_and(beyond >= 0, beyond < DEVS)
    beyond = jnp.clip(beyond, 0, DEVS - 1)
    beyond_across = across - 1 + 2 * parity
    hi, z = ind // 4, lax.rem(ind, 4)
    chunks = x_ref.shape[0] // CHUNK
    width = x_ref.shape[1] // 2

    loads = []
    for block in range(2):
        load = pltpu.make_async_copy(x_ref.at[:, pl.ds(block * width, width)], xb.at[block], r["load_sem"].at[block])
        load.start()
        loads.append(load)
    band[...] = jnp.zeros_like(band)
    mirror[...] = jnp.zeros_like(mirror)

    barrier = pltpu.get_barrier_semaphore()

    @pl.loop(0, RANKS)
    def _(other):
        pl.semaphore_signal(barrier, inc=1, device_id=(partner, other), device_id_type=MESH)

        @pl.when(other != ind)
        def _():
            pl.semaphore_signal(barrier, inc=1, device_id=(snp, other), device_id_type=MESH)

        @pl.when(has_q)
        def _():
            pl.semaphore_signal(barrier, inc=1, device_id=(across, other), device_id_type=MESH)

        @pl.when(has_beyond)
        def _():
            pl.semaphore_signal(barrier, inc=1, device_id=(beyond, other), device_id_type=MESH)

    met = 2 * RANKS - 1
    both(has_q, lambda: pl.semaphore_wait(barrier, met + 2 * RANKS), lambda: pl.semaphore_wait(barrier, met))
    for load in loads:
        load.wait()

    near_even = [1, 2, 3] if left_blocks == 1 else [2, 3]
    far_even = [2] if right_blocks == 2 else []
    pieces = [(n, s) for n in range(max(right_blocks, left_blocks)) for s in range(2)]

    def sends(n):
        return has_q if n < min(right_blocks, left_blocks) else jnp.logical_and(has_q, odd if right_blocks > n else even)

    def receives(n):
        return has_q if n < min(right_blocks, left_blocks) else jnp.logical_and(has_q, even if right_blocks > n else odd)

    def halo(n, s, c):
        rows = pl.ds(pl.multiple_of(c * CHUNK, CHUNK), CHUNK)
        half = jnp.where(odd, s, 1 - s)
        cols = pl.ds(pl.multiple_of(half * (width // 2), width // 2), width // 2)
        if right_blocks == 1 and n == 0:
            src = stage.at[rows, cols]
        else:
            src = xb.at[jnp.where(odd, 1 - n, n), rows, cols]
        at = (n * 2 + s) * chunks + c
        return pltpu.make_async_remote_copy(
            src, q.at[n, s, rows], r["halo_send"].at[at], r["halo_recv"].at[at], device_id=(across, ind), device_id_type=MESH
        )

    def start_halo(number):
        n, s, c = number // (2 * chunks), number // chunks % 2, number % chunks
        pl.when(sends(n))(lambda: halo(n, s, c).start())

    swap = [
        pltpu.make_async_remote_copy(
            xb.at[block], xb.at[2 + block], r["swap_send"].at[block], r["swap_recv"].at[block],
            device_id=(partner, ind), device_id_type=MESH,
        )
        for block in range(2)
    ]

    if right_blocks == 1:
        picked = jnp.where(odd, pick_ref[0], 0)
        for c in range(chunks):
            rows = pl.ds(c * CHUNK, CHUNK)
            stage[rows, :] = jnp.where(picked == 1, xb[1, rows, :], xb[0, rows, :])
    for number in range(len(pieces) * chunks):
        start_halo(number)
    for copy in swap:
        copy.start()

    def half_of(s):
        return jnp.where(odd, 1 - s, s)

    def tile(acc, s, t, a, b):
        cols = pl.ds(pl.multiple_of(half_of(s) * (width // 2), width // 2), width // 2)
        acc[s, :, t] = jnp.zeros((4, 64, width), F32)

        @pl.loop(0, xb.shape[1] // 1024)
        def _(k):
            rows = pl.ds(pl.multiple_of(k * 1024, 1024), 1024)
            product = lax.dot_general(
                xb[a, rows, cols], xb[b, rows, :], (((0,), (0,)), ((), ())), preferred_element_type=F32
            )
            acc[s, :, t] += product.reshape(4, 64, width)

    class Family:
        def __init__(self, name, number, even_count, odd_count):
            self.number, self.name = number, name
            self.even_count, self.odd_count = even_count, odd_count
            self.acc, self.zr, self.red, self.yr, self.rt, self.mt = (r[name + k] for k in ("acc", "zr", "red", "yr", "rt", "mt"))

        def by_parity(self, action, swapped=False):
            counts = (self.odd_count, self.even_count) if swapped else (self.even_count, self.odd_count)
            if counts[0] == counts[1]:
                action(counts[0])
                return
            if counts[0]:
                pl.when(even)(lambda: action(counts[0]))
            if counts[1]:
                pl.when(odd)(lambda: action(counts[1]))

        def z_copy(self, s, k, count):
            other = lax.rem(z + k, 4)
            at = self.number * 6 + s * 3 + k - 1
            some = pl.ds(0, count)
            return pltpu.make_async_remote_copy(
                self.acc.at[s, other, some], self.zr.at[s, 3 - k, some], r["z_send"].at[at], r["z_recv"].at[at],
                device_id=(snp, hi * 4 + other), device_id_type=MESH,
            )

        def z_start(self, s):
            def action(count):
                for k in range(1, 4):
                    self.z_copy(s, k, count).start()

            self.by_parity(action)

        def z_sum(self, s, count):
            for k in range(1, 4):
                self.z_copy(s, k, count).wait_recv()
            self.red[s, :count] = self.acc[s, z, :count] + self.zr[s, 0, :count] + self.zr[s, 1, :count] + self.zr[s, 2, :count]

        def z_drain(self, count):
            for s in range(2):
                for k in range(1, 4):
                    self.z_copy(s, k, count).wait_send()

        def turn(self, p, t, u):
            pair = jnp.concatenate([self.yr[0, t], self.yr[0, u]], axis=0)
            self.rt[:, p] = pair.T.reshape(RANKS, 64, 128)

        def y_copy(self, s, count):
            some = pl.ds(0, count)
            return pltpu.make_async_remote_copy(
                self.red.at[s, some], self.yr.at[0, some], r["y_send"].at[self.number * 2], r["y_recv"].at[self.number * 2],
                device_id=(snp, (1 - hi) * 4 + z), device_id_type=MESH,
            )

        def y_start(self, s):
            count = self.even_count
            pl.when(hi != half_of(s))(lambda: self.y_copy(s, count).start())

        def y_finish(self, s, then):
            @pl.when(hi == half_of(s))
            def _():
                self.y_copy(s, self.even_count).wait_recv()
                self.yr[0] = self.yr[0] + self.red[s]
                then()

        def drain(self):
            self.z_drain(self.even_count)
            for s in range(2):
                pl.when(hi != half_of(s))(lambda: self.y_copy(s, self.even_count).wait_send())

        def x_copy(self, s, half, source, count):
            some = pl.ds(0, count)
            return pltpu.make_async_remote_copy(
                self.red.at[s, some], self.yr.at[source, some],
                r["y_send"].at[self.number * 2 + s], r["y_recv"].at[self.number * 2 + source],
                device_id=(across, half * 4 + z), device_id_type=MESH,
            )

        def z_finish_cross(self, s):
            def action(count):
                self.z_sum(s, count)
                self.x_copy(s, half_of(s), hi, count).start()

            self.by_parity(action)

        def x_finish(self, s, then):
            @pl.when(hi == 1 - half_of(s))
            def _():
                def action(count):
                    for source in range(2):
                        self.x_copy(s, 0, source, count).wait_recv()
                    self.yr[0, :count] = self.yr[0, :count] + self.yr[1, :count]

                self.by_parity(action, swapped=True)
                then()

        def drain_cross(self):
            def action(count):
                self.z_drain(count)
                for s in range(2):
                    self.x_copy(s, half_of(s), hi, count).wait_send()

            self.by_parity(action)

        def pack_copy(self, p, kind, device, other, source):
            return pltpu.make_async_remote_copy(
                self.rt.at[other, p], self.mt.at[kind, source],
                r["pack_send"].at[(self.number * 3 + kind) * RANKS + other],
                r["pack_recv"].at[(self.number * 3 + kind) * RANKS + source],
                device_id=(device, other), device_id_type=MESH,
            )

        def pack_send(self, p, kind, device=None):
            @pl.loop(0, RANKS)
            def _(other):
                if device is None:
                    pl.when(other != ind)(lambda: self.pack_copy(p, kind, snp, other, ind).start())
                else:
                    self.pack_copy(p, kind, device, other, ind).start()

            if device is None:
                self.mt[kind, ind] = self.rt[ind, p]

        def pack_drain(self, p, kind, device=None):
            @pl.loop(0, RANKS)
            def _(other):
                if device is None:
                    pl.when(other != ind)(lambda: self.pack_copy(p, kind, snp, other, ind).wait_send())
                else:
                    self.pack_copy(p, kind, device, other, ind).wait_send()

        def pack_wait(self, kind, from_self=False):
            @pl.loop(0, RANKS)
            def _(source):
                if from_self:
                    pl.when(source != ind)(lambda: self.pack_copy(0, kind, snp, 0, source).wait_recv())
                else:
                    self.pack_copy(0, kind, partner, 0, source).wait_recv()

        def turned(self, kind, side):
            lanes = slice(64 * side, 64 * side + 64)
            return jnp.concatenate([self.mt[kind, source][:, lanes] for source in range(RANKS)], axis=1)

    inner = Family("i", 0, 5, 5)
    near = Family("a", 1, len(near_even), 4)
    far = Family("b", 2, len(far_even), 3) if left_blocks == 2 else None

    def fwd_inner():
        return pltpu.make_async_remote_copy(
            inner.yr.at[0, pl.ds(3, 2)], band.at[1, pl.ds(1, 2)], r["fwd_send"].at[0], r["fwd_recv"].at[0],
            device_id=(partner, ind), device_id_type=MESH,
        )

    def inner_places():
        own = inner.yr.at[0]
        band[0, 0] = own[0]
        mirror[0, 0] = own[0]
        band[1, 0] = own[1]
        mirror[1, 0] = own[1]
        band[0, 1] = own[2]
        inner.turn(0, 2, 2)
        inner.turn(1, 3, 4)
        inner.pack_send(0, 0)

        @pl.when(odd)
        def _():
            fwd_inner().start()
            inner.pack_send(1, 1)

        @pl.when(even)
        def _():
            band[0, 2] = own[3]
            band[0, 3] = own[4]
            inner.pack_send(1, 2, partner)

    def near_places():
        rows = near.yr.at[0]

        @pl.when(even)
        def _():
            for k in range(4):
                mirror[0, 1 + k] = rows[k]
            near.turn(0, 0, 1)
            near.turn(1, 2, 3)

        @pl.when(odd)
        def _():
            if left_blocks == 1:
                for k in range(3):
                    band[1, 2 + k] = rows[k]
                for k in range(2):
                    band[0, 3 + k] = rows[k]
                near.turn(0, 0, 0)
                near.turn(1, 1, 2)
            else:
                band[1, 3] = rows[0]
                band[1, 4] = rows[1]
                if right_blocks == 1:
                    band[0, 4] = rows[0]
                near.turn(1, 0, 1)

        near_packs("send")

    def near_packs(action):
        act = near.pack_send if action == "send" else near.pack_drain
        if left_blocks == 1:
            act(0, 0, across)
        else:
            pl.when(even)(lambda: act(0, 0, across))
        act(1, 1, beyond_across)

    def far_places():
        rows = far.yr.at[0]

        @pl.when(even)
        def _():
            for k in range(3):
                mirror[1, 2 + k] = rows[k]
            far.turn(0, 0, 1)
            far.turn(1, 2, 2)

        if right_blocks == 2:
            @pl.when(odd)
            def _():
                band[0, 4] = rows[0]
                far.turn(1, 0, 0)

        far_packs("send")

    def far_packs(action):
        act = far.pack_send if action == "send" else far.pack_drain
        pl.when(even)(lambda: act(0, 0, across))
        act(1, 1, beyond_across)

    def inner_tiles(s, waits):
        tile(inner.acc, s, 0, 0, 0)
        tile(inner.acc, s, 1, 1, 1)
        tile(inner.acc, s, 2, 0, 1)
        for copy in waits:
            copy.wait_recv()
        tile(inner.acc, s, 3, jnp.where(odd, 3, 0), jnp.where(odd, 0, 2))
        tile(inner.acc, s, 4, jnp.where(odd, 3, 0), jnp.where(odd, 1, 3))
        inner.z_start(s)

    inner_tiles(0, swap)
    inner_tiles(1, ())

    def cross(n, s, family, even_slots, odd_slots, c):
        acc = family.acc
        if c == 0:
            acc[s] = jnp.zeros(acc.shape[1:], F32)

        @pl.when(receives(n))
        def _():
            halo(n, s, c).wait_recv()
            rows = pl.ds(c * CHUNK, CHUNK)
            left = q[n, s, rows, :]

            def add(t, b):
                product = lax.dot_general(
                    left, xb[b, rows, :], (((0,), (0,)), ((), ())), preferred_element_type=F32
                )
                acc[s, :, t] += product.reshape(4, 64, width)

            for t, b in enumerate(odd_slots):
                if t < len(even_slots):
                    add(t, jnp.where(odd, b, even_slots[t]))
                else:
                    pl.when(odd)(lambda: add(t, b))


    def cross_step(index, first, last):
        n, s = pieces[index]
        family = near if n == 0 else far
        even_slots, odd_slots = (near_even, [1, 0, 3, 2]) if n == 0 else (far_even, [1, 0, 3])
        for c in range(first, last):
            cross(n, s, family, even_slots, odd_slots, c)
        if last == chunks:
            pl.when(receives(n))(lambda: family.z_start(s))

    steps = [(index, first, first + chunks // 2) for index in range(len(pieces)) for first in (0, chunks // 2)]
    near_sum = lambda s: pl.when(has_q)(lambda: near.z_finish_cross(s))
    near_end = lambda s: pl.when(has_q)(lambda: near.x_finish(s, near_places))
    far_sum = lambda s: pl.when(receives(1))(lambda: far.z_finish_cross(s))
    far_end = lambda s: pl.when(sends(1))(lambda: far.x_finish(s, far_places))
    inner_sum = lambda s: inner.z_sum(s, inner.even_count)

    def inner_out():
        for s in range(2):
            inner.y_start(s)

    def inner_end():
        for s in range(2):
            inner.y_finish(s, inner_places)

    if far is None:
        after = {
            1: [lambda: inner_sum(0)],
            2: [lambda: inner_sum(1)],
            3: [inner_out, lambda: near_sum(0), inner_end, lambda: near_end(0), lambda: near_sum(1), lambda: near_end(1)],
        }
    else:
        after = {
            1: [lambda: inner_sum(0)],
            2: [lambda: inner_sum(1)],
            3: [inner_out],
            4: [lambda: near_sum(0)],
            5: [inner_end, lambda: near_sum(1)],
            6: [lambda: far_sum(0)],
            7: [
                lambda: near_end(0), lambda: near_end(1), lambda: far_sum(1),
                lambda: far_end(0), lambda: far_end(1),
            ],
        }
    for number, step in enumerate(steps):
        cross_step(*step)
        for action in after.get(number, []):
            action()

    inner.pack_wait(0, True)
    mirror[1, 1] = inner.turned(0, 0)

    @pl.when(odd)
    def _():
        inner.pack_wait(1, True)
        mirror[0, 1] = inner.turned(1, 0)
        mirror[1, 2] = inner.turned(1, 1)
        inner.pack_wait(2)
        mirror[0, 2] = inner.turned(2, 0)
        mirror[1, 3] = inner.turned(2, 1)

    pl.when(even)(lambda: fwd_inner().wait_recv())

    @pl.when(jnp.logical_and(has_q, odd))
    def _():
        near.pack_wait(0)
        band[1, 1] = near.turned(0, 0)
        band[0, 2] = near.turned(0, 1)
        if far is not None:
            far.pack_wait(0)
            band[1, 2] = far.turned(0, 0)
            band[0, 3] = far.turned(0, 1)

    if left_blocks == 1:
        @pl.when(jnp.logical_and(has_q, even))
        def _():
            near.pack_wait(0)
            mirror[1, 2] = near.turned(0, 0)
            mirror[1, 3] = near.turned(0, 0)

    @pl.when(jnp.logical_and(has_beyond, even))
    def _():
        near.pack_wait(1)
        band[1, 3] = near.turned(1, 0)
        band[0, 4] = near.turned(1, 1)
        if far is not None:
            far.pack_wait(1)
            band[1, 4] = far.turned(1, 0)

    @pl.when(jnp.logical_and(has_beyond, odd))
    def _():
        near.pack_wait(1)
        mirror[0, 3] = near.turned(1, 0)
        mirror[1, 4] = near.turned(1, 1)
        if right_blocks == 1:
            mirror[0, 4] = near.turned(1, 0)
        else:
            far.pack_wait(1)
            mirror[0, 4] = far.turned(1, 0)

    for copy in swap:
        copy.wait_send()
    for n, s in pieces:
        for c in range(chunks):
            pl.when(sends(n))(lambda: halo(n, s, c).wait_send())
    inner.drain()
    inner.pack_drain(0, 0)

    @pl.when(odd)
    def _():
        fwd_inner().wait_send()
        inner.pack_drain(1, 1)

    pl.when(even)(lambda: inner.pack_drain(1, 2, partner))

    @pl.when(has_q)
    def _():
        near.drain_cross()
        near_packs("drain")

    if far is not None:
        pl.when(receives(1))(far.drain_cross)
        pl.when(sends(1))(lambda: far_packs("drain"))


def scratch(right_blocks, left_blocks):
    blocks = max(right_blocks, left_blocks)
    dma = lambda count: pltpu.SemaphoreType.DMA((count,))
    shapes = {
        "xb": pltpu.VMEM((4, 4096, 512), jnp.bfloat16),
        "q": pltpu.VMEM((blocks, 2, 4096, 256), jnp.bfloat16),
        "stage": pltpu.VMEM((4096 if right_blocks == 1 else 16, 512), jnp.bfloat16),
        "load_sem": dma(2),
        "swap_send": dma(2),
        "swap_recv": dma(2),
        "halo_send": dma(blocks * 16),
        "halo_recv": dma(blocks * 16),
        "z_send": dma(18),
        "z_recv": dma(18),
        "y_send": dma(6),
        "y_recv": dma(6),
        "pack_send": dma(72),
        "pack_recv": dma(72),
        "fwd_send": dma(1),
        "fwd_recv": dma(1),
    }
    families = [("i", 5, 3), ("a", 4, 2)] + ([("b", 3, 2)] if blocks == 2 else [])
    for name, count, kinds in families:
        shapes[name + "acc"] = pltpu.VMEM((2, 4, count, 64, 512), F32)
        shapes[name + "zr"] = pltpu.VMEM((2, 3, count, 64, 512), F32)
        shapes[name + "red"] = pltpu.VMEM((2, count, 64, 512), F32)
        shapes[name + "yr"] = pltpu.VMEM((1 if name == "i" else 2, count, 64, 512), F32)
        shapes[name + "rt"] = pltpu.VMEM((RANKS, 2, 64, 128), F32)
        shapes[name + "mt"] = pltpu.VMEM((kinds, RANKS, 64, 128), F32)
    return shapes


def tiles(right_blocks, left_blocks, pick, dosages):
    out = jax.ShapeDtypeStruct((2, 5, 64, 512), F32)
    return pl.pallas_call(
        functools.partial(kernel, right_blocks, left_blocks),
        out_shape=(out, out),
        in_specs=[pl.BlockSpec(memory_space=pltpu.SMEM), pl.BlockSpec(memory_space=pl.ANY)],
        out_specs=(pl.BlockSpec(memory_space=pltpu.VMEM),) * 2,
        scratch_shapes=list(scratch(right_blocks, left_blocks).values()),
        compiler_params=pltpu.CompilerParams(
            collective_id=right_blocks * 2 + left_blocks, has_side_effects=True, vmem_limit_bytes=62 << 20
        ),
        cost_estimate=pl.CostEstimate(flops=21_474_836_480, bytes_accessed=11_000_000, transcendentals=0),
        name=f"tiles_{right_blocks}_{left_blocks}",
    )(pick, dosages)


def gather_kernel(ends_ref, all_ref, mine, send_sem, recv_sem):
    snp, ind = lax.axis_index("snp"), lax.axis_index("ind")
    barrier = pltpu.get_barrier_semaphore()

    def copy(k):
        other = lax.rem(snp + k, DEVS)
        return pltpu.make_async_remote_copy(
            mine, all_ref.at[snp], send_sem.at[k], recv_sem.at[k], device_id=(other, ind), device_id_type=MESH
        )

    @pl.loop(1, DEVS)
    def _(k):
        pl.semaphore_signal(barrier, inc=1, device_id=(lax.rem(snp + k, DEVS), ind), device_id_type=MESH)

    lane = lax.broadcasted_iota(jnp.int32, (8, 128), 1)
    mine[...] = jnp.where(lane == 0, ends_ref[0], ends_ref[1])
    all_ref[snp] = mine[...]
    pl.semaphore_wait(barrier, DEVS - 1)

    @pl.loop(1, DEVS)
    def _(k):
        copy(k).start()

    @pl.loop(1, DEVS)
    def _(k):
        copy(k).wait()


def gather(window_end):
    everything = pl.pallas_call(
        gather_kernel,
        out_shape=jax.ShapeDtypeStruct((DEVS, 8, 128), jnp.int32),
        in_specs=[pl.BlockSpec(memory_space=pltpu.SMEM)],
        out_specs=pl.BlockSpec(memory_space=pltpu.VMEM),
        scratch_shapes=[
            pltpu.VMEM((8, 128), jnp.int32),
            pltpu.SemaphoreType.DMA((DEVS,)),
            pltpu.SemaphoreType.DMA((DEVS,)),
        ],
        compiler_params=pltpu.CompilerParams(collective_id=1, has_side_effects=True),
        name="gather_ends",
    )(window_end)
    return everything[:, 0, :2].reshape(-1)


def local(dosages, window_end):
    windows = gather(window_end)
    first = lax.axis_index("snp") * 2
    block = first + jnp.arange(2, dtype=jnp.int32)[:, None]
    offset = jnp.arange(5, dtype=jnp.int32)[None, :]
    band_valid = block + offset <= window_end[:, None]
    earlier = block - offset
    reach = jnp.sum(
        jnp.where(jnp.arange(32, dtype=jnp.int32) == earlier[..., None], windows, jnp.int32(0)), axis=-1, dtype=jnp.int32
    )
    mirror_valid = jnp.logical_and(earlier >= 0, block <= reach)

    reaches = (windows.reshape(8, 4) - (4 * jnp.arange(8, dtype=jnp.int32)[:, None] + 3))[:7]
    columns = jnp.max(jnp.maximum(reaches[:, 1], jnp.minimum(reaches[:, 2], reaches[:, 3])))
    choice = jnp.clip(columns - 1, 0, 2).astype(jnp.int32)
    pick = (window_end[1] >= window_end[0]).astype(jnp.int32).reshape(1)
    scale = jnp.float32(1.0 / 32768.0)

    def plan(right_blocks, left_blocks):
        def run(pick, dosages, band_valid, mirror_valid):
            band, mirror = tiles(right_blocks, left_blocks, pick, dosages)
            band = jnp.where(band_valid[..., None, None], band * scale, jnp.float32(0.0))
            mirror = jnp.where(mirror_valid[..., None, None], mirror * scale, jnp.float32(0.0))
            return lax.optimization_barrier((band, mirror))

        return run

    plans = [plan(1, 1), plan(1, 2), plan(2, 2)]
    band, mirror = lax.switch(choice, plans, pick, dosages, band_valid, mirror_valid)
    return band, mirror


def solution(mesh):
    in_specs = (P("ind", "snp"), P("snp"))
    out_specs = (P("snp", None, "ind", None), P("snp", None, "ind", None))
    return jax.shard_map(local, mesh=mesh, in_specs=in_specs, out_specs=out_specs, check_vma=False)
```

```python
import functools

import jax
import jax.numpy as jnp
from jax import lax
from jax.experimental import pallas as pl
from jax.experimental.pallas import tpu as pltpu
from jax.sharding import PartitionSpec as P

MESH = pl.DeviceIdType.MESH
F32 = jnp.float32
RANKS = 8
DEVS = 16
CHUNK = 1024


def both(condition, then, otherwise):
    pl.when(condition)(then)
    pl.when(jnp.logical_not(condition))(otherwise)


def kernel(right_blocks, left_blocks, pick_ref, x_ref, band, mirror, *refs):
    names = list(scratch(right_blocks, left_blocks))
    r = dict(zip(names, refs))
    xb, q, stage = r["xb"], r["q"], r["stage"]
    snp, ind = lax.axis_index("snp"), lax.axis_index("ind")
    odd = lax.rem(snp, 2) == 1
    even = jnp.logical_not(odd)
    parity = lax.rem(snp, 2)
    partner = snp + 1 - 2 * parity
    across = snp - 1 + 2 * parity
    has_q = jnp.logical_and(across >= 0, across < DEVS)
    across = jnp.clip(across, 0, DEVS - 1)
    beyond = snp + 2 - 4 * parity
    has_beyond = jnp.logical_and(beyond >= 0, beyond < DEVS)
    beyond = jnp.clip(beyond, 0, DEVS - 1)
    beyond_across = across - 1 + 2 * parity
    place, column = lax.rem(snp, 4), snp // 4
    diagonal = jnp.logical_or(jnp.logical_and(place == 3, snp < 12), jnp.logical_and(place == 0, snp > 0))
    relays = jnp.logical_or(jnp.logical_and(place == 1, snp < 12), jnp.logical_and(place == 2, snp > 3))
    by_way = jnp.where(odd, 3 - column, column)
    relay_to = jnp.clip(snp - 3 + 6 * parity, 0, DEVS - 1)
    hi, z = ind // 4, lax.rem(ind, 4)
    chunks = x_ref.shape[0] // CHUNK
    width = x_ref.shape[1] // 2

    loads = []
    for block in range(2):
        load = pltpu.make_async_copy(x_ref.at[:, pl.ds(block * width, width)], xb.at[block], r["load_sem"].at[block])
        load.start()
        loads.append(load)
    band[...] = jnp.zeros_like(band)
    mirror[...] = jnp.zeros_like(mirror)

    barrier = pltpu.get_barrier_semaphore()

    @pl.loop(0, RANKS)
    def _(other):
        pl.semaphore_signal(barrier, inc=1, device_id=(partner, other), device_id_type=MESH)

        @pl.when(other != ind)
        def _():
            pl.semaphore_signal(barrier, inc=1, device_id=(snp, other), device_id_type=MESH)

        @pl.when(has_q)
        def _():
            pl.semaphore_signal(barrier, inc=1, device_id=(across, other), device_id_type=MESH)

        @pl.when(has_beyond)
        def _():
            pl.semaphore_signal(barrier, inc=1, device_id=(beyond, other), device_id_type=MESH)

    involved = jnp.logical_and(jnp.logical_or(diagonal, relays), left_blocks == 1)

    @pl.when(involved)
    def _():
        greeted = jnp.where(relays, snp - 2 + 4 * parity, snp - 3 + 6 * parity)
        pl.semaphore_signal(barrier, inc=1, device_id=(greeted, ind), device_id_type=MESH)

    met = 2 * RANKS - 1
    both(
        has_q,
        lambda: both(
            involved,
            lambda: pl.semaphore_wait(barrier, met + 2 * RANKS + 1),
            lambda: pl.semaphore_wait(barrier, met + 2 * RANKS),
        ),
        lambda: pl.semaphore_wait(barrier, met),
    )
    for load in loads:
        load.wait()

    near_even = [1, 2, 3] if left_blocks == 1 else [2, 3]
    far_even = [2] if right_blocks == 2 else []
    pieces = [(n, s) for n in range(max(right_blocks, left_blocks)) for s in range(4)]
    detour = left_blocks == 1

    def sends(n):
        return has_q if n < min(right_blocks, left_blocks) else jnp.logical_and(has_q, odd if right_blocks > n else even)

    def receives(n):
        return has_q if n < min(right_blocks, left_blocks) else jnp.logical_and(has_q, even if right_blocks > n else odd)

    def quarter_of(s, flip):
        return jnp.where(flip, 3 - s, s)

    def halo(n, s, c):
        rows = pl.ds(c * CHUNK, CHUNK)
        cols = pl.ds(pl.multiple_of(quarter_of(s, even) * (width // 4), width // 4), width // 4)
        if right_blocks == 1 and n == 0:
            src = stage.at[rows, cols]
        else:
            src = xb.at[jnp.where(odd, 1 - n, n), rows, cols]
        at = (n * 4 + s) * chunks + c
        return pltpu.make_async_remote_copy(
            src, q.at[n, s, rows], r["halo_send"].at[at], r["halo_recv"].at[at], device_id=(across, ind), device_id_type=MESH
        )

    def relay_in(s, c):
        at = s * chunks + c
        src = stage.at[pl.ds(c * CHUNK, CHUNK), pl.ds(pl.multiple_of(quarter_of(s, even) * (width // 4), width // 4), width // 4)]
        return pltpu.make_async_remote_copy(
            src, r["relay"].at[s, pl.ds(c * CHUNK, CHUNK)], r["halo_send"].at[at], r["relay_recv"].at[at],
            device_id=(beyond, ind), device_id_type=MESH,
        )

    def relay_out(s, c):
        at = s * chunks + c
        rows = pl.ds(c * CHUNK, CHUNK)
        return pltpu.make_async_remote_copy(
            r["relay"].at[s, rows], q.at[0, s, rows], r["relay_send"].at[at], r["halo_recv"].at[at],
            device_id=(relay_to, ind), device_id_type=MESH,
        )

    def relayed(c):
        return c < by_way

    def start_halo(n, s, c):
        if detour and n == 0 and c < 3:
            around = jnp.logical_and(diagonal, relayed(c))
            pl.when(jnp.logical_and(sends(n), around))(lambda: relay_in(s, c).start())
            pl.when(jnp.logical_and(sends(n), jnp.logical_not(around)))(lambda: halo(n, s, c).start())
        else:
            pl.when(sends(n))(lambda: halo(n, s, c).start())

    swap = [
        pltpu.make_async_remote_copy(
            xb.at[block], xb.at[2 + block], r["swap_send"].at[block], r["swap_recv"].at[block],
            device_id=(partner, ind), device_id_type=MESH,
        )
        for block in range(2)
    ]

    if right_blocks == 1:
        picked = jnp.where(odd, pick_ref[0], 0)
        for c in range(chunks):
            rows = pl.ds(c * CHUNK, CHUNK)
            stage[rows, :] = jnp.where(picked == 1, xb[1, rows, :], xb[0, rows, :])
    for n, s in pieces:
        for c in range(chunks):
            start_halo(n, s, c)
    for copy in swap:
        copy.start()

    def half_of(s):
        return jnp.where(odd, 1 - s, s)

    def tile(acc, s, t, a, b):
        cols = pl.ds(pl.multiple_of(half_of(s) * (width // 2), width // 2), width // 2)
        acc[s, :, t] = jnp.zeros((4, 64, width), F32)

        @pl.loop(0, xb.shape[1] // 1024)
        def _(k):
            rows = pl.ds(pl.multiple_of(k * 1024, 1024), 1024)
            product = lax.dot_general(
                xb[a, rows, cols], xb[b, rows, :], (((0,), (0,)), ((), ())), preferred_element_type=F32
            )
            acc[s, :, t] += product.reshape(4, 64, width)

    class Family:
        def __init__(self, name, number, even_count, odd_count):
            self.number, self.name = number, name
            self.even_count, self.odd_count = even_count, odd_count
            self.acc = r["iacc" if name == "b" else name + "acc"]
            self.zr, self.red, self.yr, self.rt, self.mt = (r[name + k] for k in ("zr", "red", "yr", "rt", "mt"))

        def by_parity(self, action, swapped=False):
            counts = (self.odd_count, self.even_count) if swapped else (self.even_count, self.odd_count)
            if counts[0] == counts[1]:
                action(counts[0])
                return
            if counts[0]:
                pl.when(even)(lambda: action(counts[0]))
            if counts[1]:
                pl.when(odd)(lambda: action(counts[1]))

        def z_copy(self, s, k, count):
            other = lax.rem(z + k, 4)
            at = self.number * 6 + s * 3 + k - 1
            some = pl.ds(0, count)
            return pltpu.make_async_remote_copy(
                self.acc.at[s, other, some], self.zr.at[s, 3 - k, some], r["z_send"].at[at], r["z_recv"].at[at],
                device_id=(snp, hi * 4 + other), device_id_type=MESH,
            )

        def z_start(self, s, pair=None):
            def action(count):
                for k in range(1, 4):
                    if pair is None:
                        self.z_copy(s, k, count).start()
                    else:
                        pl.when(lax.rem(z + k, 4) // 2 == pair)(lambda: self.z_copy(s, k, count).start())

            self.by_parity(action)

        def z_sum(self, s, count):
            for k in range(1, 4):
                self.z_copy(s, k, count).wait_recv()
            self.red[s, :count] = self.acc[s, z, :count] + self.zr[s, 0, :count] + self.zr[s, 1, :count] + self.zr[s, 2, :count]

        def z_drain(self, count):
            for s in range(2):
                for k in range(1, 4):
                    self.z_copy(s, k, count).wait_send()

        def half_copy(self, s, side):
            rows = pl.ds(32 * side, 32)
            at = s * 2 + side
            return pltpu.make_async_remote_copy(
                self.acc.at[s, lax.rem(z + 2, 4), :, rows], self.zr.at[s, 1, :, rows],
                r["half_send"].at[at], r["half_recv"].at[at],
                device_id=(snp, hi * 4 + lax.rem(z + 1 + 2 * side, 4)), device_id_type=MESH,
            )

        def half_start(self, s):
            for side in range(2):
                self.half_copy(s, side).start()

        def half_finish(self, s):
            for side in range(2):
                self.half_copy(s, side).wait_recv()
                other = lax.rem(z + 1 + 2 * side, 4)
                rows = slice(32 * side, 32 * side + 32)
                self.acc[s, other, :, rows] = self.acc[s, other, :, rows] + self.zr[s, 1, :, rows]
                self.z_copy(s, 1 + 2 * side, self.even_count).start()

        def two_step_sum(self, s):
            for k in (1, 3):
                self.z_copy(s, k, self.even_count).wait_recv()
            self.red[s] = self.acc[s, z] + self.zr[s, 0] + self.zr[s, 2]

        def two_step_drain(self):
            for s in range(2):
                for side in range(2):
                    self.half_copy(s, side).wait_send()
                    self.z_copy(s, 1 + 2 * side, self.even_count).wait_send()

        def turn(self, p, t, u):
            pair = jnp.concatenate([self.yr[0, t], self.yr[0, u]], axis=0)
            self.rt[:, p] = pair.T.reshape(RANKS, 64, 128)

        def y_copy(self, s, count):
            some = pl.ds(0, count)
            return pltpu.make_async_remote_copy(
                self.red.at[s, some], self.yr.at[0, some], r["y_send"].at[self.number * 2], r["y_recv"].at[self.number * 2],
                device_id=(snp, (1 - hi) * 4 + z), device_id_type=MESH,
            )

        def y_start(self, s):
            count = self.even_count
            pl.when(hi != half_of(s))(lambda: self.y_copy(s, count).start())

        def y_finish(self, s, then):
            @pl.when(hi == half_of(s))
            def _():
                self.y_copy(s, self.even_count).wait_recv()
                self.yr[0] = self.yr[0] + self.red[s]
                then()

        def drain(self):
            for s in range(2):
                pl.when(hi != half_of(s))(lambda: self.y_copy(s, self.even_count).wait_send())

        def x_copy(self, s, half, source, count):
            some = pl.ds(0, count)
            return pltpu.make_async_remote_copy(
                self.red.at[s, some], self.yr.at[source, some],
                r["y_send"].at[self.number * 2 + s], r["y_recv"].at[self.number * 2 + source],
                device_id=(across, half * 4 + z), device_id_type=MESH,
            )

        def z_finish_cross(self, s):
            def action(count):
                self.z_sum(s, count)
                self.x_copy(s, half_of(s), hi, count).start()

            self.by_parity(action)

        def x_finish(self, s, then):
            @pl.when(hi == 1 - half_of(s))
            def _():
                def action(count):
                    for source in range(2):
                        self.x_copy(s, 0, source, count).wait_recv()
                    self.yr[0, :count] = self.yr[0, :count] + self.yr[1, :count]

                self.by_parity(action, swapped=True)
                then()

        def drain_cross(self):
            def action(count):
                self.z_drain(count)
                for s in range(2):
                    self.x_copy(s, half_of(s), hi, count).wait_send()

            self.by_parity(action)

        def pack_copy(self, p, kind, device, other, source):
            return pltpu.make_async_remote_copy(
                self.rt.at[other, p], self.mt.at[kind, source],
                r["pack_send"].at[(self.number * 3 + kind) * RANKS + other],
                r["pack_recv"].at[(self.number * 3 + kind) * RANKS + source],
                device_id=(device, other), device_id_type=MESH,
            )

        def pack_send(self, p, kind, device=None):
            @pl.loop(0, RANKS)
            def _(other):
                if device is None:
                    pl.when(other != ind)(lambda: self.pack_copy(p, kind, snp, other, ind).start())
                else:
                    self.pack_copy(p, kind, device, other, ind).start()

            if device is None:
                self.mt[kind, ind] = self.rt[ind, p]

        def pack_drain(self, p, kind, device=None):
            @pl.loop(0, RANKS)
            def _(other):
                if device is None:
                    pl.when(other != ind)(lambda: self.pack_copy(p, kind, snp, other, ind).wait_send())
                else:
                    self.pack_copy(p, kind, device, other, ind).wait_send()

        def pack_wait(self, kind, from_self=False):
            @pl.loop(0, RANKS)
            def _(source):
                if from_self:
                    pl.when(source != ind)(lambda: self.pack_copy(0, kind, snp, 0, source).wait_recv())
                else:
                    self.pack_copy(0, kind, partner, 0, source).wait_recv()

        def turned(self, kind, side):
            lanes = slice(64 * side, 64 * side + 64)
            return jnp.concatenate([self.mt[kind, source][:, lanes] for source in range(RANKS)], axis=1)

    inner = Family("i", 0, 5, 5)
    near = Family("a", 1, len(near_even), 4)
    far = Family("b", 2, len(far_even), 3) if left_blocks == 2 else None

    def fwd_inner():
        return pltpu.make_async_remote_copy(
            inner.yr.at[0, pl.ds(3, 2)], band.at[1, pl.ds(1, 2)], r["fwd_send"].at[0], r["fwd_recv"].at[0],
            device_id=(partner, ind), device_id_type=MESH,
        )

    def inner_places():
        own = inner.yr.at[0]
        band[0, 0] = own[0]
        mirror[0, 0] = own[0]
        band[1, 0] = own[1]
        mirror[1, 0] = own[1]
        band[0, 1] = own[2]
        inner.turn(0, 2, 2)
        inner.turn(1, 3, 4)
        inner.pack_send(0, 0)

        @pl.when(odd)
        def _():
            fwd_inner().start()
            inner.pack_send(1, 1)

        @pl.when(even)
        def _():
            band[0, 2] = own[3]
            band[0, 3] = own[4]
            inner.pack_send(1, 2, partner)

    def near_places():
        rows = near.yr.at[0]

        @pl.when(even)
        def _():
            for k in range(4):
                mirror[0, 1 + k] = rows[k]
            near.turn(0, 0, 1)
            near.turn(1, 2, 3)

        @pl.when(odd)
        def _():
            if left_blocks == 1:
                for k in range(3):
                    band[1, 2 + k] = rows[k]
                for k in range(2):
                    band[0, 3 + k] = rows[k]
                near.turn(0, 0, 0)
                near.turn(1, 1, 2)
            else:
                band[1, 3] = rows[0]
                band[1, 4] = rows[1]
                if right_blocks == 1:
                    band[0, 4] = rows[0]
                near.turn(1, 0, 1)

        near_packs("send")

    def near_packs(action):
        act = near.pack_send if action == "send" else near.pack_drain
        if left_blocks == 1:
            act(0, 0, across)
        else:
            pl.when(even)(lambda: act(0, 0, across))
        act(1, 1, beyond_across)

    def far_places():
        rows = far.yr.at[0]

        @pl.when(even)
        def _():
            for k in range(3):
                mirror[1, 2 + k] = rows[k]
            far.turn(0, 0, 1)
            far.turn(1, 2, 2)

        if right_blocks == 2:
            @pl.when(odd)
            def _():
                band[0, 4] = rows[0]
                far.turn(1, 0, 0)

        far_packs("send")

    def far_packs(action):
        act = far.pack_send if action == "send" else far.pack_drain
        pl.when(even)(lambda: act(0, 0, across))
        act(1, 1, beyond_across)

    def inner_tiles(s, waits):
        tile(inner.acc, s, 0, 0, 0)
        tile(inner.acc, s, 1, 1, 1)
        tile(inner.acc, s, 2, 0, 1)
        for copy in waits:
            copy.wait_recv()
        tile(inner.acc, s, 3, jnp.where(odd, 3, 0), jnp.where(odd, 0, 2))
        tile(inner.acc, s, 4, jnp.where(odd, 3, 0), jnp.where(odd, 1, 3))
        inner.half_start(s)

    inner_tiles(0, swap)
    inner_tiles(1, ())
    inner.half_finish(0)

    def cross(n, quarter, family, even_slots, odd_slots, c):
        s, acc = quarter // 2, family.acc
        pair = lax.rem(quarter_of(quarter, odd), 2)
        shares = pl.ds(2 * pair, 2)
        if quarter % 2 == 0 and c == 0:
            acc[s] = jnp.zeros(acc.shape[1:], F32)

        @pl.when(receives(n))
        def _():
            halo(n, quarter, c).wait_recv()
            rows = pl.ds(c * CHUNK, CHUNK)
            left = q[n, quarter, rows, :]

            def add(t, b):
                product = lax.dot_general(
                    left, xb[b, rows, :], (((0,), (0,)), ((), ())), preferred_element_type=F32
                )
                acc[s, shares, t] += product.reshape(2, 64, width)

            for t, b in enumerate(odd_slots):
                if t < len(even_slots):
                    add(t, jnp.where(odd, b, even_slots[t]))
                else:
                    pl.when(odd)(lambda: add(t, b))

    def cross_step(index):
        n, quarter = pieces[index]
        family = near if n == 0 else far
        even_slots, odd_slots = (near_even, [1, 0, 3, 2]) if n == 0 else (far_even, [1, 0, 3])
        for c in range(chunks):
            if detour and n == 0 and c < 3:
                @pl.when(jnp.logical_and(relays, relayed(c)))
                def _():
                    relay_in(quarter, c).wait_recv()
                    relay_out(quarter, c).start()

            cross(n, quarter, family, even_slots, odd_slots, c)
        pair = lax.rem(quarter_of(quarter, odd), 2)
        pl.when(receives(n))(lambda: family.z_start(quarter // 2, pair))

    near_sum = lambda s: pl.when(has_q)(lambda: near.z_finish_cross(s))
    near_end = lambda s: pl.when(has_q)(lambda: near.x_finish(s, near_places))
    far_sum = lambda s: pl.when(receives(1))(lambda: far.z_finish_cross(s))
    far_end = lambda s: pl.when(sends(1))(lambda: far.x_finish(s, far_places))
    inner_sum = inner.two_step_sum

    inner_out = inner.y_start

    def inner_end():
        for s in range(2):
            inner.y_finish(s, inner_places)

    if far is None:
        after = {
            0: [lambda: inner.half_finish(1)],
            1: [lambda: inner_sum(0), lambda: inner_out(0)],
            2: [lambda: inner_sum(1)],
            3: [
                lambda: inner_out(1), lambda: near_sum(0), lambda: near_sum(1), inner_end,
                lambda: near_end(0), lambda: near_end(1),
            ],
        }
    else:
        after = {
            0: [lambda: inner.half_finish(1)],
            1: [lambda: inner_sum(0)],
            2: [lambda: inner_sum(1), lambda: inner_out(0)],
            3: [lambda: inner_out(1), inner.two_step_drain],
            4: [lambda: near_sum(0)],
            5: [inner_end, lambda: near_sum(1)],
            6: [lambda: far_sum(0)],
            7: [
                lambda: near_end(0), lambda: near_end(1), lambda: far_sum(1),
                lambda: far_end(0), lambda: far_end(1),
            ],
        }
    for number in range(len(pieces)):
        cross_step(number)
        for action in after.get(number, []):
            action()

    inner.pack_wait(0, True)
    mirror[1, 1] = inner.turned(0, 0)

    @pl.when(odd)
    def _():
        inner.pack_wait(1, True)
        mirror[0, 1] = inner.turned(1, 0)
        mirror[1, 2] = inner.turned(1, 1)
        inner.pack_wait(2)
        mirror[0, 2] = inner.turned(2, 0)
        mirror[1, 3] = inner.turned(2, 1)

    pl.when(even)(lambda: fwd_inner().wait_recv())

    @pl.when(jnp.logical_and(has_q, odd))
    def _():
        near.pack_wait(0)
        band[1, 1] = near.turned(0, 0)
        band[0, 2] = near.turned(0, 1)
        if far is not None:
            far.pack_wait(0)
            band[1, 2] = far.turned(0, 0)
            band[0, 3] = far.turned(0, 1)

    if left_blocks == 1:
        @pl.when(jnp.logical_and(has_q, even))
        def _():
            near.pack_wait(0)
            mirror[1, 2] = near.turned(0, 0)
            mirror[1, 3] = near.turned(0, 0)

    @pl.when(jnp.logical_and(has_beyond, even))
    def _():
        near.pack_wait(1)
        band[1, 3] = near.turned(1, 0)
        band[0, 4] = near.turned(1, 1)
        if far is not None:
            far.pack_wait(1)
            band[1, 4] = far.turned(1, 0)

    @pl.when(jnp.logical_and(has_beyond, odd))
    def _():
        near.pack_wait(1)
        mirror[0, 3] = near.turned(1, 0)
        mirror[1, 4] = near.turned(1, 1)
        if right_blocks == 1:
            mirror[0, 4] = near.turned(1, 0)
        else:
            far.pack_wait(1)
            mirror[0, 4] = far.turned(1, 0)

    for copy in swap:
        copy.wait_send()
    for n, s in pieces:
        for c in range(chunks):
            pl.when(sends(n))(lambda: halo(n, s, c).wait_send())
            if detour and n == 0 and c < 3:
                pl.when(jnp.logical_and(relays, relayed(c)))(lambda: relay_out(s, c).wait_send())
    if far is None:
        inner.two_step_drain()
    inner.drain()
    inner.pack_drain(0, 0)

    @pl.when(odd)
    def _():
        fwd_inner().wait_send()
        inner.pack_drain(1, 1)

    pl.when(even)(lambda: inner.pack_drain(1, 2, partner))

    @pl.when(has_q)
    def _():
        near.drain_cross()
        near_packs("drain")

    if far is not None:
        pl.when(receives(1))(far.drain_cross)
        pl.when(sends(1))(lambda: far_packs("drain"))


def scratch(right_blocks, left_blocks):
    blocks = max(right_blocks, left_blocks)
    dma = lambda count: pltpu.SemaphoreType.DMA((count,))
    shapes = {
        "xb": pltpu.VMEM((4, 4096, 512), jnp.bfloat16),
        "q": pltpu.VMEM((blocks, 4, 4096, 128), jnp.bfloat16),
        "stage": pltpu.VMEM((4096 if right_blocks == 1 else 16, 512), jnp.bfloat16),
        "relay": pltpu.VMEM((4, 3072 if left_blocks == 1 else 16, 128), jnp.bfloat16),
        "relay_send": dma(16),
        "relay_recv": dma(16),
        "load_sem": dma(2),
        "swap_send": dma(2),
        "swap_recv": dma(2),
        "halo_send": dma(blocks * 16),
        "halo_recv": dma(blocks * 16),
        "half_send": dma(4),
        "half_recv": dma(4),
        "z_send": dma(18),
        "z_recv": dma(18),
        "y_send": dma(6),
        "y_recv": dma(6),
        "pack_send": dma(72),
        "pack_recv": dma(72),
        "fwd_send": dma(1),
        "fwd_recv": dma(1),
    }
    families = [("i", 5, 3), ("a", 4, 2)] + ([("b", 3, 2)] if blocks == 2 else [])
    for name, count, kinds in families:
        if name != "b":
            shapes[name + "acc"] = pltpu.VMEM((2, 4, count, 64, 512), F32)
        shapes[name + "zr"] = pltpu.VMEM((2, 3, count, 64, 512), F32)
        shapes[name + "red"] = pltpu.VMEM((2, count, 64, 512), F32)
        shapes[name + "yr"] = pltpu.VMEM((1 if name == "i" else 2, count, 64, 512), F32)
        shapes[name + "rt"] = pltpu.VMEM((RANKS, 2, 64, 128), F32)
        shapes[name + "mt"] = pltpu.VMEM((kinds, RANKS, 64, 128), F32)
    return shapes


def tiles(right_blocks, left_blocks, pick, dosages):
    out = jax.ShapeDtypeStruct((2, 5, 64, 512), F32)
    return pl.pallas_call(
        functools.partial(kernel, right_blocks, left_blocks),
        out_shape=(out, out),
        in_specs=[pl.BlockSpec(memory_space=pltpu.SMEM), pl.BlockSpec(memory_space=pl.ANY)],
        out_specs=(pl.BlockSpec(memory_space=pltpu.VMEM),) * 2,
        scratch_shapes=list(scratch(right_blocks, left_blocks).values()),
        compiler_params=pltpu.CompilerParams(
            collective_id=right_blocks * 2 + left_blocks, has_side_effects=True, vmem_limit_bytes=62 << 20
        ),
        cost_estimate=pl.CostEstimate(flops=21_474_836_480, bytes_accessed=11_000_000, transcendentals=0),
        name=f"tiles_{right_blocks}_{left_blocks}",
    )(pick, dosages)


def gather_kernel(ends_ref, all_ref, mine, send_sem, recv_sem):
    snp, ind = lax.axis_index("snp"), lax.axis_index("ind")
    barrier = pltpu.get_barrier_semaphore()

    def copy(k):
        other = lax.rem(snp + k, DEVS)
        return pltpu.make_async_remote_copy(
            mine, all_ref.at[snp], send_sem.at[k], recv_sem.at[k], device_id=(other, ind), device_id_type=MESH
        )

    @pl.loop(1, DEVS)
    def _(k):
        pl.semaphore_signal(barrier, inc=1, device_id=(lax.rem(snp + k, DEVS), ind), device_id_type=MESH)

    lane = lax.broadcasted_iota(jnp.int32, (8, 128), 1)
    mine[...] = jnp.where(lane == 0, ends_ref[0], ends_ref[1])
    all_ref[snp] = mine[...]
    pl.semaphore_wait(barrier, DEVS - 1)

    @pl.loop(1, DEVS)
    def _(k):
        copy(k).start()

    @pl.loop(1, DEVS)
    def _(k):
        copy(k).wait()


def gather(window_end):
    everything = pl.pallas_call(
        gather_kernel,
        out_shape=jax.ShapeDtypeStruct((DEVS, 8, 128), jnp.int32),
        in_specs=[pl.BlockSpec(memory_space=pltpu.SMEM)],
        out_specs=pl.BlockSpec(memory_space=pltpu.VMEM),
        scratch_shapes=[
            pltpu.VMEM((8, 128), jnp.int32),
            pltpu.SemaphoreType.DMA((DEVS,)),
            pltpu.SemaphoreType.DMA((DEVS,)),
        ],
        compiler_params=pltpu.CompilerParams(collective_id=1, has_side_effects=True),
        name="gather_ends",
    )(window_end)
    return everything[:, 0, :2].reshape(-1)


def local(dosages, window_end):
    windows = gather(window_end)
    first = lax.axis_index("snp") * 2
    block = first + jnp.arange(2, dtype=jnp.int32)[:, None]
    offset = jnp.arange(5, dtype=jnp.int32)[None, :]
    band_valid = block + offset <= window_end[:, None]
    earlier = block - offset
    reach = jnp.sum(
        jnp.where(jnp.arange(32, dtype=jnp.int32) == earlier[..., None], windows, jnp.int32(0)), axis=-1, dtype=jnp.int32
    )
    mirror_valid = jnp.logical_and(earlier >= 0, block <= reach)

    reaches = (windows.reshape(8, 4) - (4 * jnp.arange(8, dtype=jnp.int32)[:, None] + 3))[:7]
    columns = jnp.max(jnp.maximum(reaches[:, 1], jnp.minimum(reaches[:, 2], reaches[:, 3])))
    choice = jnp.clip(columns - 1, 0, 2).astype(jnp.int32)
    pick = (window_end[1] >= window_end[0]).astype(jnp.int32).reshape(1)
    scale = jnp.float32(1.0 / 32768.0)

    def plan(right_blocks, left_blocks):
        def run(pick, dosages, band_valid, mirror_valid):
            band, mirror = tiles(right_blocks, left_blocks, pick, dosages)
            band = jnp.where(band_valid[..., None, None], band * scale, jnp.float32(0.0))
            mirror = jnp.where(mirror_valid[..., None, None], mirror * scale, jnp.float32(0.0))
            return lax.optimization_barrier((band, mirror))

        return run

    plans = [plan(1, 1), plan(1, 2), plan(2, 2)]
    band, mirror = lax.switch(choice, plans, pick, dosages, band_valid, mirror_valid)
    return band, mirror


def solution(mesh):
    in_specs = (P("ind", "snp"), P("snp"))
    out_specs = (P("snp", None, "ind", None), P("snp", None, "ind", None))
    return jax.shard_map(local, mesh=mesh, in_specs=in_specs, out_specs=out_specs, check_vma=False)
```
